32 devices in a mesh: dp: 8 (over z, y), tensor: 4 (over x, core).
Axes of the slice: x: 2, y: 2, z: 4, core: 2. Of those that a mesh axis runs over, the one named last changes fastest.
Arguments:
- inputs: bfloat16 [6304, 768], P(('dp', 'tensor')), may hold values from -6 to 6
- cotangent: bfloat16 [6304, 768], P(('dp', 'tensor')), may hold values from -6 to 6
- expert_ids: int32 [6304, 2], P('dp'), may hold values from 0 to 15, all different within a row; in each aligned block of 788 rows (0 to 787, 788 to 1575, ...) at most 147 rows name the same one
- layer_norm_gains: float32 [2, 768], replicated, may hold values from 0.5 to 1.5
- layer_norm_biases: float32 [2, 768], replicated, may hold values from -1.2 to 1.2
- norm_moment: float32 [4, 768], replicated, may hold values from -512 to 512
- w_qkv: bfloat16 [3, 768, 768], P(None, 'dp', 'tensor'), may hold values from -0.21875 to 0.21875
- w_attn_out: bfloat16 [768, 768], P('tensor', 'dp'), may hold values from -1.25 to 1.25
- w_router: bfloat16 [768, 16], replicated, may hold values from -0.21875 to 0.21875
- w_in: bfloat16 [16, 768, 3072], P(None, 'dp', 'tensor'), may hold values from -0.21875 to 0.21875
- w_exp_out: bfloat16 [16, 3072, 768], P(None, 'tensor', 'dp'), may hold values from -0.625 to 0.625
- m_qkv: float32 [3, 768, 768], P(None, 'dp', 'tensor'), may hold values from -512 to 512
- m_attn_out: float32 [768, 768], P('tensor', 'dp'), may hold values from -96 to 96
- m_router: float32 [768, 16], replicated, may hold values from -1024 to 1024
- m_in: float32 [16, 768, 3072], P(None, 'dp', 'tensor'), may hold values from -32 to 32
- m_exp_out: float32 [16, 3072, 768], P(None, 'tensor', 'dp'), may hold values from -6 to 6
Outputs:
- output: bfloat16 [6304, 768], P(('dp', 'tensor'))
- input_grad: float32 [6304, 768], P(('dp', 'tensor'))
- norm_moment_new: float32 [4, 768], replicated
- norm_new: float32 [4, 768], replicated
- qkv_moment_new: float32 [3, 768, 768], P(None, 'dp', 'tensor')
- qkv_new: float32 [3, 768, 768], P(None, 'dp', 'tensor')
- attn_out_moment_new: float32 [768, 768], P('tensor', 'dp')
- attn_out_new: float32 [768, 768], P('tensor', 'dp')
- router_moment_new: float32 [768, 16], replicated
- router_new: float32 [768, 16], replicated
- in_moment_new: float32 [16, 768, 3072], P(None, 'dp', 'tensor')
- in_new: float32 [16, 768, 3072], P(None, 'dp', 'tensor')
- exp_out_moment_new: float32 [16, 3072, 768], P(None, 'tensor', 'dp')
- exp_out_new: float32 [16, 3072, 768], P(None, 'tensor', 'dp')
The draws below stay inside these ranges and needn't reach their ends.
Inputs may be any that keep to these rules, and one draw needn't show every extreme that they name: `expert_ids`: within each aligned block of 788 rows (the tokens of one index of dp) no expert is named by more than 147 rows, a bound that some block reaches; the 2 ids of a row differ.
All inputs are finite; a program needn't handle non-finite values.
Results may differ from the reference program's by a relative error of at most 0.018.
Values may be sent and summed in bfloat16 or wider, within the bound.
A program may use at most 320 MiB of HBM per device.

```python
import math
import jax
import jax.numpy as jnp
import numpy as np
from jax import lax

D = 768
HEADS = 12
HD = 64
FF = 3072
EXPERTS = 16
TOPK = 2
SEQ = 197
IMGS = 4
GROUP = 788
TOKENS = 6304
CAP = 147
N_DP = 8


def level_of(rng, extent, shards, low, high):
    gain, own = 1.0, jax.random.fold_in(rng, 6)
    for dim, blocks in shards:
        heights = jnp.exp(jax.random.uniform(jax.random.fold_in(own, dim), (blocks,), jnp.float32, low / len(shards), high / len(shards)))
        gain = gain * jnp.repeat(heights, extent[dim] // blocks).reshape([-1 if axis == dim else 1 for axis in range(len(extent))])
    return gain


def shared_out(rng, own, number, rows, count, top, reach, lean):
    order = jax.random.permutation(rng, count)
    packed, usual = load_shares(count, rows * top, reach, lean, True), load_shares(count, rows * top, reach, lean, False)
    places = jnp.arange(count)

    def named(sizes, offset_by):
        used = int((sizes > 0).sum())
        fixed = max(1, used // 4)
        passed = fixed + (places - fixed + offset_by * (used - fixed)) % max(1, count - fixed)
        return jnp.zeros((count,), jnp.int32).at[order[jnp.where(places < fixed, places, passed)]].set(jnp.asarray(sizes, jnp.int32))

    sizes = jnp.where(number % 4 == 0, named(packed, number // 4), named(usual, number - number // 4 - 1))
    mixed = jax.random.permutation(jax.random.fold_in(own, 3), count)
    source_of, receiver = mixed[0:count // 2 * 2:2], mixed[1:count // 2 * 2:2]
    margin = jnp.minimum(sizes[source_of] - 1, reach - sizes[receiver]) // 2
    margin = jnp.where((source_of == order[0]) | (receiver == order[0]) | (sizes[receiver] == 0), 0, jnp.maximum(margin, 0))
    passed = jax.random.randint(jax.random.fold_in(own, 4), (count // 2,), 0, 1 << 20) % (margin + 1)
    sizes = sizes.at[source_of].add(-passed).at[receiver].add(passed)
    members = jnp.searchsorted(jnp.cumsum(sizes), jnp.arange(rows * top), side="right").astype(jnp.int32)
    listing = members.reshape(top, rows).T
    listing = listing[jax.random.permutation(jax.random.fold_in(own, 1), rows)]
    offset_by = jax.random.randint(jax.random.fold_in(own, 2), (rows, 1), 0, top)
    return jnp.take_along_axis(listing, (jnp.arange(top)[None, :] + offset_by) % top, axis=1)


def load_shares(amount, total, most, lean, full):
    weights = [(1 << 20) // math.isqrt(standing ** lean) + 1 for standing in range(1, amount + 1)]
    largest = most if full else min(most, max(-(-total // amount), total * weights[0] // sum(weights)))
    least = 1 if total - largest >= amount - 1 else 0
    holding, surplus = [largest] + [least] * (amount - 1), total - largest - least * (amount - 1)
    while surplus > 0:
        movable = [i for i in range(1, amount) if holding[i] < largest] or [i for i in range(1, amount) if holding[i] < most]
        mass, budget = sum([weights[i] for i in movable]), surplus
        for i in movable:
            extra = min(most - holding[i], max(1, budget * weights[i] // mass), surplus)
            holding[i] = holding[i] + extra
            surplus = surplus - extra
    return np.array(holding)


def scatter_about(stream_key, dims, spread, bound, cuts=(), kind=jnp.bfloat16):
    result = jax.random.normal(stream_key, dims, jnp.float32) * spread
    if len(cuts) > 0:
        result = level_of(stream_key, dims, cuts, -0.22, 0.18) * result
    return jnp.clip(result, min=-bound, max=bound).astype(kind)


def setup_inputs(seed: int = 0) -> dict:
    seeds = jax.random.split(jax.random.key(seed), 17)
    inputs = scatter_about(seeds[0], (TOKENS, D), 1.0, 6.0, ((0, 32),))
    cotangent = scatter_about(seeds[1], (TOKENS, D), 1.0, 6.0, ((0, 32),))
    expert_ids_keys = jax.random.split(jax.random.fold_in(seeds[2], 1), TOKENS // GROUP)
    expert_ids_turns = jax.random.permutation(jax.random.fold_in(seeds[2], 3), TOKENS // GROUP)
    expert_ids = jax.vmap(lambda own, number: shared_out(jax.random.fold_in(seeds[2], 2), own, number, GROUP, EXPERTS, TOPK, CAP, 2))(expert_ids_keys, expert_ids_turns).reshape((TOKENS, TOPK))
    layer_norm_gains = jnp.clip(1.0 + 0.1 * jax.random.normal(seeds[3], (2, D), jnp.float32), 0.5, 1.5)
    layer_norm_biases = scatter_about(seeds[4], (2, D), 0.2, 1.2, (), jnp.float32)
    norm_moment = scatter_about(seeds[5], (4, D), (TOKENS ** 0.5), 512.0, (), jnp.float32)
    w_qkv = scatter_about(seeds[6], (3, D, D), D ** -0.5, 0.21875, ((1, 8), (2, 4)))
    w_attn_out = scatter_about(seeds[7], (D, D), (D // 32) ** -0.5, 1.25, ((0, 4), (1, 8)))
    w_router = scatter_about(seeds[8], (D, EXPERTS), D ** -0.5, 0.21875)
    w_in = scatter_about(seeds[9], (EXPERTS, D, FF), D ** -0.5, 0.21875, ((1, 8), (2, 4)))
    w_exp_out = scatter_about(seeds[10], (EXPERTS, FF, D), (FF // 36) ** -0.5, 0.625, ((1, 4), (2, 8)))
    m_qkv = scatter_about(seeds[11], (3, D, D), (TOKENS ** 0.5), 512.0, ((1, 8), (2, 4)), jnp.float32)
    m_attn_out = scatter_about(seeds[12], (D, D), (TOKENS ** 0.5 * 0.2), 96.0, ((0, 4), (1, 8)), jnp.float32)
    m_router = scatter_about(seeds[13], (D, EXPERTS), (TOKENS ** 0.5 * 2), 1024.0, (), jnp.float32)
    m_in = scatter_about(seeds[14], (EXPERTS, D, FF), ((TOKENS * TOPK // EXPERTS) ** 0.5 * 0.2), 32.0, ((1, 8), (2, 4)), jnp.float32)
    m_exp_out = scatter_about(seeds[15], (EXPERTS, FF, D), ((TOKENS * TOPK // EXPERTS) ** 0.5 * 0.08), 6.0, ((1, 4), (2, 8)), jnp.float32)
    return dict(inputs=inputs, cotangent=cotangent, expert_ids=expert_ids, layer_norm_gains=layer_norm_gains, layer_norm_biases=layer_norm_biases, norm_moment=norm_moment, w_qkv=w_qkv, w_attn_out=w_attn_out, w_router=w_router, w_in=w_in, w_exp_out=w_exp_out, m_qkv=m_qkv, m_attn_out=m_attn_out, m_router=m_router, m_in=m_in, m_exp_out=m_exp_out)


@jax.custom_vjp
def low(v):
    return lax.optimization_barrier(v.astype(jnp.bfloat16)).astype(jnp.float32)

@jax.custom_vjp
def low_back(v):
    return v

def low_keep(v):
    return (low(v), None)

def low_pass(kept, grad):
    return (grad,)

def back_keep(v):
    return (v, None)

def back_low(kept, grad):
    return (low(grad),)
low.defvjp(low_keep, low_pass)
low_back.defvjp(back_keep, back_low)
HIGH = lax.Precision.HIGHEST
LN_EPS = 1e-06
NS_EPS = 1e-07
NS_A = 3.4445
NS_B = -4.775
NS_C = 2.0315
DECAY = 0.5
VEC_RATE = 0.0002

def apply_layer_norm(values, gain_row, offset_row):
    centre = values - lax.optimization_barrier(jnp.mean(values, axis=-1, keepdims=True))
    inv_std = lax.rsqrt(lax.optimization_barrier(jnp.mean(centre * centre, axis=-1, keepdims=True)) + LN_EPS)
    return centre * inv_std * gain_row + offset_row

def route_slots(picked):
    flat_ids = picked.reshape(-1).astype(jnp.int32)
    entries = flat_ids.shape[0]
    labels = jnp.arange(EXPERTS, dtype=jnp.int32)
    onehot = (flat_ids[:, None] == labels[None, :]).astype(jnp.int32)
    running = (jnp.cumsum(onehot, axis=0) - 1).astype(jnp.int32)
    places = lax.optimization_barrier(jnp.sum(running * onehot, axis=1)).astype(jnp.int32)
    target_slot = (flat_ids * CAP + places).astype(jnp.int32)
    sources = jnp.full((EXPERTS * CAP,), entries, jnp.int32).at[target_slot].set(jnp.arange(entries, dtype=jnp.int32))
    return (target_slot, sources)

def group_forward(params, group):
    gains, offsets, w_qkv, w_attn_out, w_router, w_in, w_exp_out = params
    rows, picked = group
    first_normalized = low(apply_layer_norm(rows, gains[0], offsets[0]))
    qkv_all = low(low_back(jnp.einsum('td,sde->ste', first_normalized, w_qkv, precision=HIGH)))
    split = qkv_all.reshape(3, IMGS, SEQ, HEADS, HD)
    scores = low_back(jnp.einsum('bqhe,bkhe->bhqk', split[0], split[1], precision=HIGH) * HD ** (-0.5))
    weights = low(jax.nn.softmax(scores, axis=-1))
    mixed = jnp.einsum('bhqk,bkhe->bqhe', weights, split[2], precision=HIGH).reshape(GROUP, D)
    mixed = low(low_back(mixed))
    attended = low_back(jnp.dot(mixed, w_attn_out, precision=HIGH))
    residual_midpoint = rows + attended
    second_normalized = low(apply_layer_norm(residual_midpoint, gains[1], offsets[1]))
    logits = low_back(jnp.dot(second_normalized, w_router, precision=HIGH))
    router_probs = jax.nn.softmax(logits, axis=-1)
    gates = jnp.take_along_axis(router_probs, picked.astype(jnp.int32), axis=1)
    target_slot, sources = route_slots(picked)
    token_of_slot = jnp.where(sources < GROUP * TOPK, sources // TOPK, GROUP).astype(jnp.int32)
    padded = jnp.concatenate([second_normalized, jnp.zeros((1, D), second_normalized.dtype)], 0)
    expert_rows = padded[token_of_slot].reshape(EXPERTS, CAP, D)
    pre_act = low_back(jnp.einsum('ecd,edf->ecf', expert_rows, w_in, precision=HIGH))
    activated = low(jax.nn.gelu(pre_act, approximate=False))
    expert_out = low_back(jnp.einsum('ecf,efd->ecd', activated, w_exp_out, precision=HIGH)).reshape(EXPERTS * CAP, D)
    picked_out = expert_out[target_slot].reshape(GROUP, TOPK, D)
    combined = low_back(lax.optimization_barrier(jnp.sum(gates[:, :, None] * picked_out, axis=1)))
    return residual_midpoint + combined

def orthogonalize(matrix):
    norm_value = jnp.sqrt(jnp.sum(matrix * matrix))
    current = matrix / (norm_value + NS_EPS)
    for repeat in range(5):
        square = jnp.dot(current, current.T, precision=HIGH)
        poly_term = NS_B * square + NS_C * jnp.dot(square, square, precision=HIGH)
        current = NS_A * current + jnp.dot(poly_term, current, precision=HIGH)
    return current

def reference(inputs, cotangent, expert_ids, layer_norm_gains, layer_norm_biases, norm_moment, w_qkv, w_attn_out, w_router, w_in, w_exp_out, m_qkv, m_attn_out, m_router, m_in, m_exp_out):
    params = tuple((item.astype(jnp.float32) for item in (layer_norm_gains, layer_norm_biases, w_qkv, w_attn_out, w_router, w_in, w_exp_out)))
    groups_in = inputs.astype(jnp.float32).reshape(N_DP, GROUP, D)
    groups_ids = expert_ids.reshape(N_DP, GROUP, TOPK)
    checked = jax.checkpoint(group_forward)

    def forward(rows_all, *weights_all):

        def scan_body(carry, group):
            return (carry, checked(weights_all, group))
        unused, results = lax.scan(scan_body, jnp.zeros((), jnp.float32), (rows_all, groups_ids))
        return results
    out_groups, pullback = jax.vjp(forward, groups_in, *params)
    gradients = pullback(cotangent.astype(jnp.float32).reshape(N_DP, GROUP, D))
    output = out_groups.reshape(TOKENS, D).astype(jnp.bfloat16)
    input_grad = gradients[0].reshape(TOKENS, D)
    grad_gain, grad_bias, grad_qkv, grad_out, grad_router, grad_in, grad_exp = gradients[1:]
    vec_grad = jnp.concatenate([grad_gain, grad_bias], 0)
    vec_params = jnp.concatenate([params[0], params[1]], 0)
    norm_moment_new = DECAY * norm_moment + vec_grad
    norm_new = vec_params - VEC_RATE * norm_moment_new
    qkv_moment_new = DECAY * m_qkv + grad_qkv
    attn_out_moment_new = DECAY * m_attn_out + grad_out
    router_moment_new = DECAY * m_router + grad_router
    in_moment_new = DECAY * m_in + grad_in
    exp_out_moment_new = DECAY * m_exp_out + grad_exp
    oriented = qkv_moment_new.transpose(1, 0, 2).reshape(D, 3 * D)
    ortho_qkv = orthogonalize(oriented).reshape(D, 3, D).transpose(1, 0, 2)
    ortho_out = orthogonalize(attn_out_moment_new.T).T
    ortho_router = orthogonalize(router_moment_new.T).T
    ortho_in = lax.map(orthogonalize, in_moment_new)
    ortho_exp = jnp.swapaxes(lax.map(orthogonalize, jnp.swapaxes(exp_out_moment_new, 1, 2)), 1, 2)
    qkv_new = params[2] - math.sqrt(3.0) * ortho_qkv
    attn_out_new = params[3] - ortho_out
    router_new = params[4] - ortho_router
    in_new = params[5] - math.sqrt(max(1.0, FF / D)) * ortho_in
    exp_out_new = params[6] - ortho_exp
    return (output, input_grad, norm_moment_new, norm_new, qkv_moment_new, qkv_new, attn_out_moment_new, attn_out_new, router_moment_new, router_new, in_moment_new, in_new, exp_out_moment_new, exp_out_new)
```

```python
import math

import jax
import jax.numpy as jnp
from jax import lax
from jax.experimental import pallas as pl
from jax.experimental.pallas import tpu as pltpu
from jax.sharding import PartitionSpec as P

D = 768
HD = 64
FF = 3072
CAP = 147
EXPERTS = 16
SEQ = 197

HIGH = lax.Precision.HIGHEST
LN_EPS = 1e-06
NS_EPS = 1e-07
NS_A = 3.4445
NS_B = -4.775
NS_C = 2.0315
DECAY = 0.5
VEC_RATE = 0.0002
INV_ROOT_TWO = 0.7071067811865476
INV_ROOT_TWO_PI = 0.3989422804014327
BF = jnp.bfloat16
F32 = jnp.float32


def mm(spec, left, right):
    return jnp.einsum(spec, left, right, preferred_element_type=F32)


def after(value, other):
    return lax.optimization_barrier((value, other))[0]


def apply_layer_norm(values, gain_row, offset_row):
    centre = values - jnp.mean(values, axis=-1, keepdims=True)
    inv_std = lax.rsqrt(jnp.mean(centre * centre, axis=-1, keepdims=True) + LN_EPS)
    normed = centre * inv_std
    return (normed * gain_row + offset_row, normed, inv_std)


def norm_back(grad_normed, normed, inv_std, gain_row):
    scaled = grad_normed * gain_row
    first_mean = jnp.mean(scaled, axis=-1, keepdims=True)
    second_mean = jnp.mean(scaled * normed, axis=-1, keepdims=True)
    grad_values = inv_std * (scaled - first_mean - normed * second_mean)
    gain_grad = jnp.sum(grad_normed * normed, axis=0, keepdims=True)
    return (grad_values, gain_grad, jnp.sum(grad_normed, axis=0, keepdims=True))


def local_orthogonalize(matrix):
    norm_value = jnp.sqrt(jnp.sum(matrix * matrix))
    current = matrix / (norm_value + NS_EPS)
    for repeat in range(5):
        square = jnp.dot(current, current.T, precision=HIGH)
        poly_term = NS_B * square + NS_C * jnp.dot(square, square, precision=HIGH)
        current = NS_A * current + jnp.dot(poly_term, current, precision=HIGH)
    return current


def orthogonalize(matrix):
    wide = matrix.astype(F32)
    inverse = 1.0 / (jnp.sqrt(jnp.sum(wide * wide)) + NS_EPS)
    rows = matrix.shape[0]
    unit = (
        lax.broadcasted_iota(jnp.int32, (rows, rows), 0)
        == lax.broadcasted_iota(jnp.int32, (rows, rows), 1)
    ).astype(F32)
    current = matrix
    for repeat in range(5):
        square = mm("ic,jc->ij", current, current)
        if repeat == 0:
            square = square * (inverse * inverse)
        rest = (square - unit).astype(BF)
        poly = (
            (NS_A - NS_C) * unit + (NS_B + 2.0 * NS_C) * square + NS_C * mm("ij,jk->ik", rest, rest)
        ).astype(BF)
        grown = mm("ij,jc->ic", poly, current)
        if repeat == 0:
            grown = grown * inverse
        current = grown.astype(BF)
    return current


def dot(left, right, left_dim, right_dim):
    return lax.dot_general(
        left, right, (((left_dim,), (right_dim,)), ((), ())), preferred_element_type=F32
    )


class Ortho:
    def __init__(self, current, square, rest, poly, size):
        self.current, self.square, self.rest, self.poly, self.size = (
            current, square, rest, poly, size
        )
        self.n = square.shape[0]
        self.blocks, self.w = current.shape[0], current.shape[-1]
        self.tile = 256
        self.cuts = [(i, i + self.tile) for i in range(0, self.n, self.tile)]

    def unit(self, first, last):
        shape = (last - first, self.n - first)
        return (
            lax.broadcasted_iota(jnp.int32, shape, 0) == lax.broadcasted_iota(jnp.int32, shape, 1)
        ).astype(F32)

    def clear(self):
        self.square[...] = jnp.zeros_like(self.square)

    def add_square(self, b):
        block = self.current[b].reshape(self.n, self.w)
        for first, last in self.cuts:
            self.square[first:last, first:] += dot(block[first:last, :], block[first:, :], 1, 1)

    def make_poly(self):
        square, rest, poly, cuts = self.square, self.rest, self.poly, self.cuts
        scale = self.size[...]
        scale_two = scale * scale
        for first, last in cuts:
            for low, high in cuts:
                if low > first:
                    square[low:high, first:last] = square[first:last, low:high].T
        for first, last in cuts:
            if first > 0:
                rest[first:last, :first] = (square[first:last, :first] * scale_two).astype(BF)
            rest[first:last, first:] = (
                square[first:last, first:] * scale_two - self.unit(first, last)
            ).astype(BF)
        for first, last in cuts:
            strip = scale * (
                (NS_A - NS_C) * self.unit(first, last)
                + (NS_B + 2.0 * NS_C) * scale_two * square[first:last, first:]
                + NS_C * dot(rest[first:last, :], rest[:, first:], 1, 0)
            )
            poly[first:last, first:] = strip.astype(BF)
            for low, high in cuts:
                if low > first:
                    poly[low:high, first:last] = strip[:, low - first : high - first].T.astype(BF)

    def measure(self):
        total = jnp.zeros((1, 1), F32)
        for first, last in self.cuts:
            diagonal = self.unit(first, last)[:, : self.tile] * self.square[first:last, first:last]
            total = total + jnp.sum(
                jnp.sum(diagonal, axis=1, keepdims=True), axis=0, keepdims=True
            )
        self.size[...] = 1.0 / (jnp.sqrt(total) + NS_EPS)

    def grown(self, b):
        block = self.current[b].reshape(self.n, self.w)
        return dot(self.poly[...], block, 1, 0).astype(BF)

    def steps(self):
        self.measure()

        @pl.loop(0, 4)
        def _(step):
            self.make_poly()
            self.size[...] = jnp.ones((1, 1), F32)
            self.clear()

            @pl.loop(0, self.blocks)
            def _(b):
                self.current[b] = self.grown(b).reshape(self.current.shape[1:])
                self.add_square(b)

        self.make_poly()


def ortho_kernel(x_ref, current, poly, square, rest, size):
    ortho = Ortho(current, square, rest, poly, size)
    ortho.clear()

    @pl.loop(0, ortho.blocks)
    def _(b):
        current[b] = x_ref[b]
        ortho.add_square(b)

    ortho.steps()


def ortho_call(blocks):
    count, n, w = blocks.shape
    vmem = pl.BlockSpec(memory_space=pltpu.VMEM)
    return pl.pallas_call(
        ortho_kernel,
        out_shape=(jax.ShapeDtypeStruct((count, n, w), BF), jax.ShapeDtypeStruct((n, n), BF)),
        in_specs=[vmem],
        out_specs=(vmem, vmem),
        scratch_shapes=[
            pltpu.VMEM((n, n), F32), pltpu.VMEM((n, n), BF), pltpu.VMEM((1, 1), F32)
        ],
        cost_estimate=pl.CostEstimate(
            flops=20 * count * n * n * w, bytes_accessed=4 * count * n * w, transcendentals=0
        ),
        compiler_params=pltpu.CompilerParams(vmem_limit_bytes=50 * 1024 * 1024),
        name="orthogonalize",
    )(blocks)


MESH = pl.DeviceIdType.MESH
PEERS = (4, 1, 5, 2, 6, 3, 7)


def experts_kernel(
    slots_ref, win_ref, wexp_ref,
    came_ref, gin_ref, gexp_ref,
    rows, weights, part, other, rows_of, hidden_of,
    tok_send, tok_recv, fwd_send, fwd_recv, sum_send, sum_recv, ret_send, ret_recv,
    wx_send, wx_recv, load_sem,
):
    n_experts, n_t, n_dp, pair, width = rows.shape
    quarter = pair // 2
    share = gin_ref.shape[2]
    d, t = lax.axis_index("dp"), lax.axis_index("tensor")
    sibling, across = (d, t ^ 1), (d, t ^ 2)
    count = n_dp * quarter

    def remote(source, target, send, recv, device):
        return pltpu.make_async_remote_copy(
            src_ref=source, dst_ref=target, send_sem=send, recv_sem=recv,
            device_id=device, device_id_type=MESH,
        )

    def tok(e, k):
        return remote(
            slots_ref.at[d ^ k, e], rows.at[e, 0, k],
            tok_send.at[e, k], tok_recv.at[e, k], (d ^ k, t),
        )

    def tok_own(e):
        return pltpu.make_async_copy(slots_ref.at[d, e], rows.at[e, 0, 0], tok_recv.at[e, 0])

    def forward(kind, e, k):
        source, target = ((0, 1), (0, 2), (2, 3))[kind]
        return remote(
            rows.at[e, source, k], rows.at[e, target, k],
            fwd_send.at[kind, e, k], fwd_recv.at[kind, e, k],
            across if kind == 1 else sibling,
        )

    def partial(stage, e):
        return remote(
            part.at[e, 3 - stage], other.at[e, stage],
            sum_send.at[stage, e], sum_recv.at[stage, e],
            across if stage == 1 else sibling,
        )

    def ret(e, k):
        return remote(
            part.at[e, 0, k], came_ref.at[d, e],
            ret_send.at[e, k], ret_recv.at[e, k], (d ^ k, t),
        )

    def ret_own(e):
        return pltpu.make_async_copy(part.at[e, 0, 0], came_ref.at[d, e], ret_recv.at[e, 0])

    def load(e):
        return pltpu.make_async_copy(win_ref.at[:, e], weights.at[0, e], load_sem.at[e])

    def second(e, k):
        return remote(
            wexp_ref.at[d ^ k, e], weights.at[1, e, d], wx_send.at[e, k], wx_recv.at[e, k], (d ^ k, t)
        )

    def second_own(e):
        return pltpu.make_async_copy(wexp_ref.at[d, e], weights.at[1, e, d], wx_recv.at[e, 0])

    def send(e):
        for k in PEERS:
            tok(e, k).start()
        for k in PEERS:
            second(e, k).start()

    def wait_second(e):
        second_own(e).wait()

        @pl.loop(1, n_dp)
        def _(k):
            second(e, k).wait_recv()

    barrier = pltpu.get_barrier_semaphore()

    @pl.loop(1, n_dp)
    def _(k):
        pl.semaphore_signal(barrier, inc=1, device_id=(d ^ k, t), device_id_type=MESH)

    pl.semaphore_signal(barrier, inc=1, device_id=sibling, device_id_type=MESH)
    pl.semaphore_signal(barrier, inc=1, device_id=across, device_id_type=MESH)
    for e in range(n_experts):
        tok_own(e).start()
        load(e).start()
        second_own(e).start()
    pl.semaphore_wait(barrier, n_dp + 1)
    send(0)

    def pass_on(e):
        for k in (0,) + PEERS:
            if k == 0:
                tok_own(e).wait()
            else:
                tok(e, k).wait_recv()
            forward(0, e, k).start()
            forward(1, e, k).start()

    def pass_again(e):
        for k in (0,) + PEERS:
            forward(1, e, k).wait_recv()
            forward(2, e, k).start()

        @pl.loop(0, n_dp)
        def _(k):
            forward(0, e, k).wait_recv()
            forward(2, e, k).wait_recv()

    def give_back(e):
        partial(1, e).wait_recv()
        partial(2, e).wait_recv()
        for k in range(n_dp):
            part[e, 0, k] = (
                part[e, 0, k].astype(F32) + other[e, 1, k].astype(F32) + other[e, 2, k].astype(F32)
            ).astype(BF)
        ret_own(e).start()
        for k in PEERS:
            ret(e, k).start()

    def weight_grads(e):
        gin_ref[:, e] = dot(rows_of[0], hidden_of[1], 0, 0).astype(BF).reshape(n_dp, share, width)
        gexp_ref[:, e] = dot(rows_of[1], hidden_of[0], 0, 0).astype(BF).reshape(n_dp, share, width)

    pass_on(0)
    send(1)
    pass_again(0)
    wait_second(0)
    for e in range(n_experts):
        load(e).wait()

    @pl.loop(0, n_experts * n_t)
    def _(step):
        e = step // n_t
        r = n_t - 1 - step % n_t
        w_in = weights[0, e].reshape(width, width)
        w_exp = weights[1, e].reshape(width, width)
        pairs = [rows[e, r, k].astype(F32) for k in range(n_dp)]
        act_rows = jnp.concatenate([block[:quarter] for block in pairs], axis=0).astype(BF)
        grad_rows = jnp.concatenate([block[quarter:] for block in pairs], axis=0).astype(BF)
        pre = dot(act_rows, w_in, 1, 0)
        normal = 0.5 * (1.0 + lax.erf(pre * INV_ROOT_TWO))
        slope = normal + pre * jnp.exp(-0.5 * pre * pre) * INV_ROOT_TWO_PI
        act = (pre * normal).astype(BF)
        grad_pre = (dot(grad_rows, w_exp, 1, 0) * slope).astype(BF)
        at = pl.ds(pl.multiple_of(r * count, count), count)
        rows_of[0, at] = act_rows
        rows_of[1, at] = grad_rows
        hidden_of[0, at] = act
        hidden_of[1, at] = grad_pre
        row_out, row_grad = dot(act, w_exp, 1, 1), dot(grad_pre, w_in, 1, 1)
        for k in range(n_dp):
            own = slice(k * quarter, (k + 1) * quarter)
            part[e, r, k] = jnp.concatenate([row_out[own], row_grad[own]], axis=0).astype(BF)

        @pl.when(r == n_t - 1)
        def _():
            partial(0, e).start()

        @pl.when(r == 2)
        def _():
            partial(0, e).wait_recv()
            for k in range(n_dp):
                part[e, 2, k] = (
                    part[e, 2, k].astype(F32) + other[e, 0, k].astype(F32)
                ).astype(BF)
            partial(1, e).start()

        @pl.when(r == 1)
        def _():
            partial(2, e).start()

        @pl.when(step == n_t - 1)
        def _():
            pass_on(1)
            weight_grads(0)
            give_back(0)
            pass_again(1)
            wait_second(1)

        @pl.when(step == 2 * n_t - 1)
        def _():
            weight_grads(1)
            give_back(1)

    for e in range(n_experts):
        ret_own(e).wait()
        for stage in range(3):
            partial(stage, e).wait_send()

        @pl.loop(0, n_dp)
        def _(k, e=e):
            for kind in range(3):
                forward(kind, e, k).wait_send()

        @pl.loop(1, n_dp)
        def _(k, e=e):
            tok(e, k).wait_send()
            second(e, k).wait_send()
            ret(e, k).wait_send()
            ret(e, k).wait_recv()


def experts_call(slots, w_in, w_exp):
    n_dp, n_experts, pair, width = slots.shape
    share = w_in.shape[2]
    n_t = lax.axis_size("tensor")
    anywhere = pl.BlockSpec(memory_space=pl.ANY)
    vmem = pl.BlockSpec(memory_space=pltpu.VMEM)
    grads = jax.ShapeDtypeStruct((n_dp, n_experts, share, width), BF)
    dma = pltpu.SemaphoreType.DMA
    part = (n_experts, n_t, n_dp, pair, width)
    rows = n_experts * n_t * n_dp * pair
    return pl.pallas_call(
        experts_kernel,
        out_shape=(jax.ShapeDtypeStruct(slots.shape, BF), grads, grads),
        in_specs=[anywhere] * 3,
        out_specs=(anywhere, vmem, vmem),
        scratch_shapes=[
            pltpu.VMEM(part, BF),
            pltpu.VMEM((2, n_experts, n_dp, share, width), BF),
            pltpu.VMEM(part, BF),
            pltpu.VMEM((n_experts, 3) + part[2:], BF),
            pltpu.VMEM((2, n_t * n_dp * pair // 2, width), BF),
            pltpu.VMEM((2, n_t * n_dp * pair // 2, width), BF),
            dma((n_experts, n_dp)),
            dma((n_experts, n_dp)),
            dma((3, n_experts, n_dp)),
            dma((3, n_experts, n_dp)),
            dma((3, n_experts)),
            dma((3, n_experts)),
            dma((n_experts, n_dp)),
            dma((n_experts, n_dp)),
            dma((n_experts, n_dp)),
            dma((n_experts, n_dp)),
            dma((n_experts,)),
        ],
        cost_estimate=pl.CostEstimate(
            flops=40 * rows * width * width, bytes_accessed=400_000_000, transcendentals=0
        ),
        compiler_params=pltpu.CompilerParams(
            collective_id=1, has_side_effects=True, vmem_limit_bytes=60 * 1024 * 1024
        ),
        name="experts",
    )(slots, w_in, w_exp)


def layer_norm_parts(values):
    centre = values - jnp.mean(values, axis=-1, keepdims=True)
    inv_std = lax.rsqrt(jnp.mean(centre * centre, axis=-1, keepdims=True) + LN_EPS)
    return centre * inv_std, inv_std


def remote(source, target, send, recv, device):
    return pltpu.make_async_remote_copy(
        src_ref=source, dst_ref=target, send_sem=send, recv_sem=recv,
        device_id=device, device_id_type=MESH,
    )


def greet(n_dp, d, t, more=0):
    barrier = pltpu.get_barrier_semaphore()

    @pl.loop(1, n_dp)
    def _(k):
        pl.semaphore_signal(barrier, inc=1, device_id=(d ^ k, t), device_id_type=MESH)

    pl.semaphore_signal(barrier, inc=1, device_id=(d, t ^ 1), device_id_type=MESH)
    pl.semaphore_signal(barrier, inc=1, device_id=(d, t ^ 2), device_id_type=MESH)
    pl.semaphore_wait(barrier, n_dp + 1 + more)


class Gather:
    def __init__(self, blocks, send, recv, d, t):
        self.copies = [
            remote(blocks.at[i], blocks.at[i], send.at[n], recv.at[n], (d, t ^ hop))
            for n, (i, hop) in enumerate(((t, 1), (t, 2), (t ^ 2, 1)))
        ]

    def start(self):
        self.copies[0].start()
        self.copies[1].start()

    def pass_on(self):
        self.copies[1].wait_recv()
        self.copies[2].start()

    def finish(self):
        self.copies[0].wait_recv()
        self.copies[2].wait_recv()

    def wait_sent(self):
        for copy in self.copies:
            copy.wait_send()


class Scatter:
    def __init__(self, block, landed, send, recv, d, t):
        self.block, self.landed = block, landed
        self.copies = [
            remote(block(3 - n), landed.at[n], send.at[n], recv.at[n], (d, t ^ hop))
            for n, hop in enumerate((1, 2, 1))
        ]

    def send(self, r):
        if r == 2:
            self.copies[0].wait_recv()
            own = self.block(2)
            own[...] = (own[...].astype(F32) + self.landed[0].astype(F32)).astype(BF)
        self.copies[3 - r].start()

    def total(self):
        self.copies[1].wait_recv()
        self.copies[2].wait_recv()
        return (
            self.block(0)[...].astype(F32)
            + self.landed[1].astype(F32)
            + self.landed[2].astype(F32)
        )

    def wait_sent(self):
        for copy in self.copies:
            copy.wait_send()


class Exchange:
    def __init__(self, blocks, target, send, recv, d, t):
        self.n_dp = blocks.shape[0]
        self.parts = (blocks, target, send, recv, d, t)

    def copy(self, k):
        blocks, target, send, recv, d, t = self.parts
        return remote(blocks.at[d ^ k], target.at[d], send.at[k], recv.at[k], (d ^ k, t))

    def own(self):
        blocks, target, send, recv, d, t = self.parts
        return pltpu.make_async_copy(blocks.at[d], target.at[d], recv.at[0])

    def start(self):
        self.own().start()
        for k in PEERS:
            self.copy(k).start()

    def finish(self):
        self.own().wait()

        @pl.loop(1, self.n_dp)
        def _(k):
            self.copy(k).wait_recv()

    def wait_sent(self):
        @pl.loop(1, self.n_dp)
        def _(k):
            self.copy(k).wait_send()


class Spread:
    def __init__(self, source, blocks, send, recv, d, t):
        self.own = pltpu.make_async_copy(source, blocks.at[d], recv.at[0])
        self.first = [
            remote(source, blocks.at[d], send.at[k], recv.at[k], (d ^ k, t)) for k in (1, 2, 4, 6)
        ]
        self.onward = [
            remote(blocks.at[d ^ k], blocks.at[d ^ k], send.at[k ^ 1], recv.at[k ^ 1], (d ^ 1, t))
            for k in (2, 4, 6)
        ]

    def start(self):
        self.own.start()
        for copy in (self.first[2], self.first[3], self.first[1], self.first[0]):
            copy.start()

    def finish(self):
        for n in range(3):
            self.first[n + 1].wait_recv()
            self.onward[n].start()
        self.own.wait()
        self.first[0].wait_recv()
        for copy in self.onward:
            copy.wait_recv()

    def wait_sent(self):
        for copy in self.first + self.onward:
            copy.wait_send()


def of_head(block, head):
    lane = lax.broadcasted_iota(jnp.int32, block.shape, 1)
    return jnp.where(lane // HD == head, block, jnp.zeros_like(block))


def head_probs(query, key, head):
    scores = dot(of_head(query, head), key, 1, 1) * HD ** (-0.5)
    seen = lax.broadcasted_iota(jnp.int32, scores.shape, 1) < SEQ
    scores = jnp.where(seen, scores, -1e30)
    expo = jnp.exp(scores - jnp.max(scores, axis=-1, keepdims=True))
    return expo / jnp.sum(expo, axis=-1, keepdims=True)


def only_tokens(block):
    row = lax.broadcasted_iota(jnp.int32, block.shape, 0)
    return jnp.where(row < SEQ, block, jnp.zeros_like(block))


def front_kernel(
    local_heads,
    x_ref, cot_ref, wp_ref, gains_ref, biases_ref, ids_ref, wr_ref, win_ref,
    a1_out, three_out, mixed_out, w_out, slots_out, middle_ref, cots_ref, gate_ref, slot_ref, win_out,
    a1, cot, a2, three, mixed, w, part, landed, slots,
    wt_send, wt_recv, in_send, in_recv,
    ag_send, ag_recv, sum_send, sum_recv, out_sem,
):
    n_dp, share, wide = w.shape
    n_t, rows, width = a1.shape
    third = width // 3
    d, t = lax.axis_index("dp"), lax.axis_index("tensor")
    greet(n_dp, d, t)

    weights = Spread(wp_ref, w, wt_send, wt_recv, d, t)
    weights.start()
    gathers = [Gather(ref, ag_send.at[n], ag_recv.at[n], d, t) for n, ref in enumerate((a1, cot, a2))]
    x = x_ref[...].astype(F32)
    normed, _ = layer_norm_parts(x)
    a1[t] = only_tokens(normed * gains_ref[0:1, :] + biases_ref[0:1, :]).astype(BF)
    cot[t] = cot_ref[...]
    gathers[0].start()
    gathers[1].start()
    gathers[0].pass_on()
    gathers[0].finish()
    weights.finish()
    bulk_in = Exchange(win_ref, win_out, in_send, in_recv, d, t)
    bulk_in.start()

    experts, quarter = wr_ref.shape[0], slots.shape[2] // 2
    label = lax.broadcasted_iota(jnp.int32, (experts, rows), 0)
    earlier = (
        lax.broadcasted_iota(jnp.int32, (rows, rows), 0)
        < lax.broadcasted_iota(jnp.int32, (rows, rows), 1)
    ).astype(BF)
    taken = jnp.zeros((experts, 1), F32)
    first_place = (t * quarter).astype(F32)
    chosen = []
    for image in range(n_t):
        named = [label == ids_ref[image, k : k + 1, :] for k in range(2)]
        chosen.append(named)
        counted = named[0].astype(F32) + named[1].astype(F32)
        before = taken + dot(counted.astype(BF), earlier, 1, 0)
        taken = taken + jnp.sum(counted, axis=1, keepdims=True)
        for k in range(2):
            place = jnp.sum(jnp.where(named[k], before, 0.0), axis=0, keepdims=True) - first_place
            ids = ids_ref[image, k : k + 1, :].astype(F32)
            mine = (place >= 0.0) & (place < quarter) & (ids >= 0.0)
            slot_ref[image, k : k + 1, :] = jnp.where(mine, ids * quarter + place, -1.0)

    sums = Scatter(lambda r: part.at[r], landed, sum_send, sum_recv, d, t)
    for r in reversed(range(n_t)):
        image = t ^ r
        every = w[...].reshape(n_dp * share, wide)
        qkv = dot(a1[image], every[:, :width], 1, 0).astype(BF)
        three[image] = qkv
        query, key, value = [qkv[:, s * third : (s + 1) * third] for s in range(3)]
        heads = jnp.zeros((rows, third), F32)
        for head in range(local_heads):
            probs = head_probs(query, key, head).astype(BF)
            heads = heads + dot(probs, of_head(value, head), 1, 0)
        mixed[image] = heads.astype(BF)
        part[r] = dot(mixed[image], every[:, width:], 1, 1).astype(BF)
        if r > 0:
            sums.send(r)
        if r == 1:
            gathers[1].pass_on()
    middle = x + only_tokens(sums.total())
    middle_ref[...] = middle
    normed, _ = layer_norm_parts(middle)
    a2[t] = only_tokens(normed * gains_ref[1:2, :] + biases_ref[1:2, :]).astype(BF)
    gathers[2].start()
    outs = [
        pltpu.make_async_copy(source, target, out_sem.at[n])
        for n, (source, target) in enumerate(
            ((a1, a1_out), (three, three_out), (mixed, mixed_out), (w, w_out), (slots, slots_out))
        )
    ]
    for out in outs[:4]:
        out.start()
    gathers[1].finish()
    gathers[2].pass_on()
    gathers[2].finish()

    gates = []
    for image in range(n_t):
        logits = dot(wr_ref[...], a2[image], 1, 1)
        expo = jnp.exp(logits - jnp.max(logits, axis=0, keepdims=True))
        probs = expo / jnp.sum(expo, axis=0, keepdims=True)
        gates.append(
            [jnp.sum(jnp.where(chosen[image][k], probs, 0.0), axis=0, keepdims=True) for k in range(2)]
        )
    pairs = slots.shape[1]
    held = pairs * quarter

    @pl.loop(0, n_dp)
    def _(host):
        number = lax.broadcasted_iota(jnp.int32, (held, rows), 0) + host * held
        number = number.astype(F32)
        slot_act = jnp.zeros((held, width), F32)
        slot_cot = jnp.zeros((held, width), F32)
        gate = jnp.zeros((held, 1), F32)
        for image in range(n_t):
            picks = [slot_ref[image, k : k + 1, :] == number for k in range(2)]
            spread = jnp.where(picks[0] | picks[1], 1.0, 0.0).astype(BF)
            slot_act = slot_act + dot(spread, a2[image], 1, 0)
            slot_cot = slot_cot + dot(spread, cot[image], 1, 0)
            for k in range(2):
                gate = gate + jnp.sum(
                    jnp.where(picks[k], gates[image][k], 0.0), axis=1, keepdims=True
                )
        slot_grad = gate * slot_cot
        gate_ref[host] = gate
        cots_ref[host] = slot_cot.astype(BF)
        for e in range(pairs):
            own = slice(e * quarter, (e + 1) * quarter)
            slots[host, e] = jnp.concatenate([slot_act[own], slot_grad[own]], axis=0).astype(BF)

    outs[4].start()
    for out in outs:
        out.wait()
    weights.wait_sent()
    sums.wait_sent()
    for gather in gathers:
        gather.wait_sent()
    bulk_in.finish()
    bulk_in.wait_sent()


def front_call(x, cot, wp, gains, biases, ids, w_router, w_in, quarter, local_heads):
    n_dp, n_t = w_in.shape[0], lax.axis_size("tensor")
    rows, width = x.shape
    share, wide = wp.shape
    anywhere = pl.BlockSpec(memory_space=pl.ANY)
    vmem = pl.BlockSpec(memory_space=pltpu.VMEM)
    dma = pltpu.SemaphoreType.DMA

    def shape(*dims, kind=BF):
        return jax.ShapeDtypeStruct(dims, kind)

    group = (n_t, rows, width)
    pairs = w_in.shape[1]
    slots = (n_dp, pairs, 2 * quarter, width)
    return pl.pallas_call(
        lambda *refs: front_kernel(local_heads, *refs),
        out_shape=(
            shape(*group), shape(*group), shape(n_t, rows, width // 3), shape(n_dp, share, wide),
            shape(*slots), shape(rows, width, kind=F32), shape(n_dp, pairs * quarter, width),
            shape(n_dp, pairs * quarter, 1, kind=F32), shape(n_t, 2, rows, kind=F32),
            shape(*w_in.shape),
        ),
        in_specs=[vmem, vmem, anywhere, vmem, vmem, vmem, vmem, anywhere],
        out_specs=(anywhere,) * 5 + (vmem,) * 4 + (anywhere,),
        scratch_shapes=[pltpu.VMEM(group, BF)] * 4
        + [
            pltpu.VMEM((n_t, rows, width // 3), BF),
            pltpu.VMEM((n_dp, share, wide), BF),
            pltpu.VMEM(group, BF),
            pltpu.VMEM((n_t - 1, rows, width), BF),
            pltpu.VMEM(slots, BF),
        ]
        + [dma((n_dp,))] * 4
        + [dma((3, 3)), dma((3, 3)), dma((3,)), dma((3,)), dma((5,))],
        cost_estimate=pl.CostEstimate(
            flops=4 * n_t * rows * width * wide, bytes_accessed=400_000_000, transcendentals=0
        ),
        compiler_params=pltpu.CompilerParams(
            collective_id=2, has_side_effects=True, vmem_limit_bytes=50 * 1024 * 1024
        ),
        name="front",
    )(x, cot, wp, gains, biases, ids, w_router, w_in)


def back_kernel(
    local_heads, experts,
    came_ref, cots_ref, gate_ref, slot_ref, middle_ref, x_ref, cot_ref, gains_ref, biases_ref, wr_ref,
    a1_ref, three_ref, mixed_ref, w_ref, min_ref, mexp_ref, gin_ref, gexp_ref,
    output_ref, input_grad_ref, attn_ref, small_ref, min_out, mexp_out, gin_out, gexp_out,
    tok, cols, tok_landed, gm, part, landed, grads, sum_three, sum_out, shares,
    in_send, in_recv, exp_send, exp_recv, at_send, at_recv,
    ag_send, ag_recv, tok_send, tok_recv, sum_send, sum_recv,
):
    n_dp, share, wide = w_ref.shape
    n_t, rows, width = a1_ref.shape
    third = width // 3
    d, t = lax.axis_index("dp"), lax.axis_index("tensor")
    greet(n_dp, d, t)
    bulks = [
        Exchange(min_ref, min_out, in_send, in_recv, d, t),
        Exchange(mexp_ref, mexp_out, exp_send, exp_recv, d, t),
    ]
    for bulk in bulks:
        bulk.start()

    pairs, quarter = came_ref.shape[1], came_ref.shape[2] // 2
    held = pairs * quarter

    @pl.loop(0, n_dp)
    def _(host):
        at = pl.ds(pl.multiple_of(host * held, held), held)
        came = [came_ref[host, e].astype(F32) for e in range(pairs)]
        slot_out = jnp.concatenate([block[:quarter] for block in came], axis=0)
        row_grad = jnp.concatenate([block[quarter:] for block in came], axis=0)
        gate_grad = jnp.sum(cots_ref[host].astype(F32) * slot_out, axis=1, keepdims=True)
        lane = lax.broadcasted_iota(jnp.int32, (held, 128), 1) - host * pairs
        row = lax.broadcasted_iota(jnp.int32, (held, 128), 0)
        named = (row >= lane * quarter) & (row < (lane + 1) * quarter)
        cols[at, :width] = (gate_ref[host] * slot_out).astype(BF)
        cols[at, width : 2 * width] = row_grad.astype(BF)
        cols[at, 2 * width :] = jnp.where(
            named, jnp.broadcast_to(gate_grad, named.shape), 0.0
        ).astype(BF)

    tokens = Scatter(lambda r: tok.at[t ^ r], tok_landed, tok_send, tok_recv, d, t)
    number = lax.broadcasted_iota(jnp.int32, (cols.shape[0], rows), 0).astype(F32)
    for r in reversed(range(n_t)):
        image = t ^ r
        picks = [slot_ref[image, k : k + 1, :] == number for k in range(2)]
        spread = jnp.where(picks[0] | picks[1], 1.0, 0.0).astype(BF)
        tok[image] = dot(spread, cols[...], 0, 0).astype(BF)
        if r > 0:
            tokens.send(r)
    middle = middle_ref[...]
    gain_two = gains_ref[1:2, :]
    normed_two, inverse_two = layer_norm_parts(middle)
    act_two = only_tokens(normed_two * gain_two + biases_ref[1:2, :]).astype(BF)
    logits = dot(act_two, wr_ref[...], 1, 0)
    logits = jnp.where(lax.broadcasted_iota(jnp.int32, logits.shape, 1) < experts, logits, -1e30)
    expo = jnp.exp(logits - jnp.max(logits, axis=-1, keepdims=True))
    probs = expo / jnp.sum(expo, axis=-1, keepdims=True)
    total = tokens.total()
    output_ref[...] = (middle + total[:, :width]).astype(BF)
    grad_probs = total[:, 2 * width :]
    grad_logits = probs * (grad_probs - jnp.sum(probs * grad_probs, axis=-1, keepdims=True))
    grad_logits = only_tokens(grad_logits).astype(BF)
    second_grad = only_tokens(total[:, width : 2 * width]) + dot(grad_logits, wr_ref[...], 1, 1)
    grad_middle, gain_two_grad, bias_two_grad = norm_back(
        second_grad, normed_two, inverse_two, gain_two
    )
    grad_middle = only_tokens(grad_middle + cot_ref[...].astype(F32))
    input_grad_ref[...] = grad_middle
    gm[t] = grad_middle.astype(BF)
    gather = Gather(gm, ag_send, ag_recv, d, t)
    gather.start()
    small_ref[...] = jnp.zeros_like(small_ref)
    small_ref[1:2, :] = gain_two_grad
    small_ref[3:4, :] = bias_two_grad
    small_ref[4 : 4 + experts, :] = dot(grad_logits, act_two, 0, 0)[:experts]
    sum_three[...] = jnp.zeros_like(sum_three)
    sum_out[...] = jnp.zeros_like(sum_out)
    gather.pass_on()
    gather.finish()

    sums = Scatter(lambda r: part.at[r], landed, sum_send, sum_recv, d, t)
    for r in reversed(range(n_t)):
        image = t ^ r
        every = w_ref[...].reshape(n_dp * share, wide)
        grad_rows = gm[image]
        qkv = three_ref[image]
        query, key, value = [qkv[:, s * third : (s + 1) * third] for s in range(3)]
        grad_mixed = dot(grad_rows, every[:, width:], 1, 0).astype(BF)
        grad_query = jnp.zeros((rows, third), F32)
        grad_key = jnp.zeros((rows, third), F32)
        grad_value = jnp.zeros((rows, third), F32)
        for head in range(local_heads):
            head_weights = head_probs(query, key, head)
            grad_head = of_head(grad_mixed, head)
            grad_weights = dot(grad_head, value, 1, 1)
            delta = jnp.sum(head_weights * grad_weights, axis=-1, keepdims=True)
            grad_scores = (head_weights * (grad_weights - delta)).astype(BF)
            grad_query = grad_query + dot(grad_scores, of_head(key, head), 1, 0)
            grad_key = grad_key + dot(grad_scores, of_head(query, head), 0, 0)
            grad_value = grad_value + dot(head_weights.astype(BF), grad_head, 0, 0)
        grad_three = jnp.concatenate(
            [
                (grad_query * HD ** (-0.5)).astype(BF),
                (grad_key * HD ** (-0.5)).astype(BF),
                grad_value.astype(BF),
            ],
            axis=1,
        )
        part[r] = dot(grad_three, every[:, :width], 1, 1).astype(BF)
        if r > 0:
            sums.send(r)
        sum_three[...] += dot(a1_ref[image], grad_three, 0, 0)
        sum_out[...] += dot(grad_rows, mixed_ref[image], 0, 0)
    grads[:, :, :width] = sum_three[...].astype(BF).reshape(n_dp, share, width)
    grads[:, :, width:] = sum_out[...].astype(BF).reshape(n_dp, share, third)
    over_y = [
        remote(
            grads.at[d ^ 1 ^ (2 * i)], shares.at[i], at_send.at[i], at_recv.at[i], (d ^ 1, t)
        )
        for i in range(4)
    ]
    along_z = [
        remote(
            shares.at[i], shares.at[4 + i], at_send.at[4 + i], at_recv.at[4 + i], (d ^ (2 * i), t)
        )
        for i in range(1, 4)
    ]
    for copy in over_y:
        copy.start()

    for i in (2, 3, 1, 0):
        over_y[i].wait_recv()
        shares[i] = (shares[i].astype(F32) + grads[d ^ (2 * i)].astype(F32)).astype(BF)
        if i > 0:
            along_z[i - 1].start()

    first_grad = only_tokens(sums.total())
    normed_one, inverse_one = layer_norm_parts(x_ref[...].astype(F32))
    grad_in, gain_one_grad, bias_one_grad = norm_back(
        first_grad, normed_one, inverse_one, gains_ref[0:1, :]
    )
    input_grad_ref[...] += grad_in
    small_ref[0:1, :] = gain_one_grad
    small_ref[2:3, :] = bias_one_grad
    total = shares[0].astype(F32)
    for i in range(1, 4):
        along_z[i - 1].wait_recv()
        total = total + shares[4 + i].astype(F32)
    attn_ref[...] = total
    for copy in over_y + along_z:
        copy.wait_send()
    gather.wait_sent()
    tokens.wait_sent()
    sums.wait_sent()
    for bulk in bulks:
        bulk.finish()
        bulk.wait_sent()


def back_call(
    came, cots, gate, slot, middle, x, cot, gains, biases, w_router, a1, three, mixed, w,
    m_in, m_exp, g_in, g_exp, local_heads, experts,
):
    n_dp, share, wide = w.shape
    n_t, rows, width = a1.shape
    anywhere = pl.BlockSpec(memory_space=pl.ANY)
    vmem = pl.BlockSpec(memory_space=pltpu.VMEM)
    dma = pltpu.SemaphoreType.DMA
    small_rows = -(-(4 + experts) // 8) * 8
    cols = 2 * width + 128
    return pl.pallas_call(
        lambda *refs: back_kernel(local_heads, experts, *refs),
        out_shape=(
            jax.ShapeDtypeStruct((rows, width), BF),
            jax.ShapeDtypeStruct((rows, width), F32),
            jax.ShapeDtypeStruct((share, wide), F32),
            jax.ShapeDtypeStruct((small_rows, width), F32),
        )
        + (jax.ShapeDtypeStruct(m_exp.shape, BF),) * 4,
        in_specs=[vmem] * 14 + [anywhere] * 4,
        out_specs=(vmem,) * 4 + (anywhere,) * 4,
        input_output_aliases={16: 6, 17: 7},
        scratch_shapes=[
            pltpu.VMEM((n_t, rows, cols), BF),
            pltpu.VMEM((experts * came.shape[2] // 2, cols), BF),
            pltpu.VMEM((n_t - 1, rows, cols), BF),
            pltpu.VMEM((n_t, rows, width), BF),
            pltpu.VMEM((n_t, rows, width), BF),
            pltpu.VMEM((n_t - 1, rows, width), BF),
            pltpu.VMEM((n_dp, share, wide), BF),
            pltpu.VMEM((width, width), F32),
            pltpu.VMEM((width, width // 3), F32),
            pltpu.VMEM((n_dp, share, wide), BF),
        ]
        + [dma((n_dp,))] * 6
        + [dma((3,))] * 6,
        cost_estimate=pl.CostEstimate(
            flops=20 * n_t * rows * width * wide, bytes_accessed=300_000_000, transcendentals=0
        ),
        compiler_params=pltpu.CompilerParams(
            collective_id=3, has_side_effects=True, vmem_limit_bytes=56 * 1024 * 1024
        ),
        name="back",
    )(
        came, cots, gate, slot, middle, x, cot, gains, biases, w_router, a1, three, mixed, w,
        m_in, m_exp, g_in, g_exp,
    )


def last_kernel(
    min_ref, mexp_ref, gin_ref, gexp_ref, pay_ref,
    ortho_ref, gin_out, gexp_out, all_out, small_ref,
    held, grown, moments, current, pays, alls, square, rest, poly, size,
    load_sem, pay_send, pay_recv, in_send, in_recv, exp_send, exp_recv,
    mat_send, mat_recv, ag_send, ag_recv, out_sem,
):
    n_dp, n_experts, share, width = gin_ref.shape
    n_t = moments.shape[0]
    d, t = lax.axis_index("dp"), lax.axis_index("tensor")
    loads = []
    for q in range(n_t):
        kind, e = divmod(q, n_experts)
        for n, (source, target) in enumerate(
            (((min_ref, mexp_ref)[kind], held), ((gin_ref, gexp_ref)[kind], grown))
        ):
            loads.append(
                pltpu.make_async_copy(source.at[:, e], target.at[q], load_sem.at[n, q])
            )
    for load in loads:
        load.start()
    barrier = pltpu.get_barrier_semaphore()
    pl.semaphore_signal(barrier, inc=1, device_id=(d, t ^ 3), device_id_type=MESH)
    greet(n_dp, d, t, 1)

    pay = Spread(pay_ref, pays, pay_send, pay_recv, d, t)
    pay.start()
    bulks = [
        Exchange(gin_ref, gin_out, in_send, in_recv, d, t),
        Exchange(gexp_ref, gexp_out, exp_send, exp_recv, d, t),
    ]
    for bulk in bulks:
        bulk.start()
    for load in loads:
        load.wait()

    @pl.loop(0, n_t)
    def _(q):
        for k in range(n_dp):
            moments[q, k] = (DECAY * held[q, k].astype(F32) + grown[q, k].astype(F32)).astype(BF)

    def matrix(step):
        return remote(
            moments.at[t ^ step], current.at[step],
            mat_send.at[step], mat_recv.at[step], (d, t ^ step),
        )

    own_matrix = pltpu.make_async_copy(moments.at[t], current.at[0], mat_recv.at[0])
    own_matrix.start()
    for step in (2, 3, 1):
        matrix(step).start()

    pay.finish()
    total = jnp.zeros((pays.shape[1] - share, width), F32)
    for k in range(n_dp):
        alls[t, k * share : (k + 1) * share] = pays[k, :share]
        total = total + pays[k, share:].astype(F32)
    alls[t, n_dp * share :] = total.astype(BF)
    gather = Gather(alls, ag_send, ag_recv, d, t)

    ortho = Ortho(current, square, rest, poly, size)
    ortho.clear()
    own_matrix.wait()
    ortho.add_square(0)
    matrix(1).wait_recv()
    ortho.add_square(1)
    gather.start()
    for step in (2, 3):
        matrix(step).wait_recv()
        ortho.add_square(step)
    ortho.steps()
    gather.pass_on()
    for b in range(n_t):
        block = ortho.grown(b)
        for k in range(n_dp):
            ortho_ref[k, t ^ b] = block[k * share : (k + 1) * share]
    gather.finish()
    out = pltpu.make_async_copy(alls, all_out, out_sem)
    out.start()
    small = jnp.zeros(small_ref.shape, F32)
    for b in range(n_t):
        small = small + alls[b, n_dp * share :].astype(F32)
    small_ref[...] = small
    out.wait()
    gather.wait_sent()
    for step in range(1, n_t):
        matrix(step).wait_send()

    pay.wait_sent()
    for bulk in bulks:
        bulk.finish()
        bulk.wait_sent()


def last_call(m_in, m_exp, g_in, g_exp, pay):
    n_dp, n_experts, share, width = g_in.shape
    n_t = lax.axis_size("tensor")
    anywhere = pl.BlockSpec(memory_space=pl.ANY)
    vmem = pl.BlockSpec(memory_space=pltpu.VMEM)
    dma = pltpu.SemaphoreType.DMA
    mats = pltpu.VMEM((n_t, n_dp, share, width), BF)
    every = (n_t, n_dp * share + pay.shape[0] - share, width)
    bulk = jax.ShapeDtypeStruct(g_in.shape, BF)
    return pl.pallas_call(
        last_kernel,
        out_shape=(
            jax.ShapeDtypeStruct((n_dp, n_t, share, width), BF),
            bulk,
            bulk,
            jax.ShapeDtypeStruct(every, BF),
            jax.ShapeDtypeStruct((pay.shape[0] - share, width), F32),
        ),
        in_specs=[anywhere] * 5,
        out_specs=(vmem, anywhere, anywhere, anywhere, vmem),
        scratch_shapes=[
            mats,
            mats,
            mats,
            mats,
            pltpu.VMEM((n_dp,) + pay.shape, BF),
            pltpu.VMEM(every, BF),
            pltpu.VMEM((width, width), F32),
            pltpu.VMEM((width, width), BF),
            pltpu.VMEM((width, width), BF),
            pltpu.VMEM((1, 1), F32),
            dma((2, n_t)),
        ]
        + [dma((n_dp,))] * 6
        + [dma((n_t,))] * 2
        + [dma((3,))] * 2
        + [dma],
        cost_estimate=pl.CostEstimate(
            flops=80 * width * width * width, bytes_accessed=300_000_000, transcendentals=0
        ),
        compiler_params=pltpu.CompilerParams(
            collective_id=4, has_side_effects=True, vmem_limit_bytes=58 * 1024 * 1024
        ),
        name="last",
    )(m_in, m_exp, g_in, g_exp, pay)


def local(
    inputs,
    cotangent,
    expert_ids,
    layer_norm_gains,
    layer_norm_biases,
    norm_moment,
    w_qkv,
    w_attn_out,
    w_router,
    w_in,
    w_exp_out,
    m_qkv,
    m_attn_out,
    m_router,
    m_in,
    m_exp_out,
):
    rows, width = inputs.shape
    group_rows, top_count = expert_ids.shape
    experts, share, hidden = w_in.shape
    head_cols = w_attn_out.shape[0]
    n_dp = lax.axis_size("dp")
    n_t = lax.axis_size("tensor")
    t_index = lax.axis_index("tensor")
    d_index = lax.axis_index("dp")
    per_host = experts // n_dp
    rows_pad = -(-rows // 16) * 16
    quarter = -(-(-(-CAP // n_t)) // 8) * 8
    third = width // 3

    def padded(block):
        return jnp.pad(block, ((0, rows_pad - rows), (0, 0)))

    def by_host(shard):
        return shard.reshape(n_dp, per_host, share, hidden)

    def pack_attention(three, out):
        return jnp.concatenate([three[0], three[1], three[2], out.T], axis=1)

    blocks = pack_attention(w_qkv, w_attn_out).reshape(share, 4, head_cols)
    blocks = jnp.pad(blocks, ((0, 0), (0, 0), (0, third - head_cols))).reshape(share, 4 * third)
    x_pad, cot_pad = padded(inputs), padded(cotangent)
    ids = jnp.pad(
        expert_ids.reshape(n_t, rows, top_count).transpose(0, 2, 1),
        ((0, 0), (0, 0), (0, rows_pad - rows)),
        constant_values=-1,
    )
    act_one_group, three, mixed, attn_weights, slot_pair, middle, cots, gate, slot, sent_in = front_call(
        x_pad,
        cot_pad,
        blocks,
        layer_norm_gains,
        layer_norm_biases,
        ids,
        w_router.T,
        by_host(w_in),
        quarter,
        head_cols // HD,
    )
    came, in_grad_parts, exp_grad_parts = experts_call(
        slot_pair, sent_in, by_host(jnp.swapaxes(w_exp_out, 1, 2))
    )

    results = back_call(
        came,
        cots,
        gate,
        slot,
        middle,
        x_pad,
        cot_pad,
        layer_norm_gains,
        layer_norm_biases,
        jnp.pad(w_router, ((0, 0), (0, 128 - experts))),
        act_one_group,
        three,
        mixed,
        attn_weights,
        by_host(m_in.astype(BF)),
        by_host(jnp.swapaxes(m_exp_out.astype(BF), 1, 2)),
        in_grad_parts,
        exp_grad_parts,
        head_cols // HD,
        experts,
    )
    output, input_grad, attn_sum, small_part = results[:4]
    sent_m_in, sent_m_exp, in_grad_parts, exp_grad_parts = results[4:]
    output, input_grad = output[:rows], input_grad[:rows]
    attn_sum = attn_sum.reshape(share, 4, third)[:, :, :head_cols].reshape(share, width)

    attn_moment = DECAY * pack_attention(m_qkv, m_attn_out) + attn_sum
    attn_blocks = attn_moment.reshape(share, 4, head_cols)
    qkv_moment_new = attn_blocks[:, :3].transpose(1, 0, 2)
    attn_out_moment_new = attn_blocks[:, 3].T
    pay_rows = -(-small_part.shape[0] // 16) * 16
    small_part = jnp.pad(small_part, ((0, pay_rows - small_part.shape[0]), (0, 0)))
    pay = jnp.concatenate([attn_moment, small_part], 0).astype(BF)

    ortho, in_grad, exp_grad, gathered, small = last_call(
        sent_m_in, sent_m_exp, in_grad_parts, exp_grad_parts, pay
    )
    ortho = lax.all_to_all(
        ortho.reshape(n_dp * n_t, share, hidden),
        ("dp", "tensor"),
        split_axis=0,
        concat_axis=0,
        tiled=True,
    )
    ortho = ortho.reshape(n_dp, 2, per_host, share, hidden).transpose(1, 0, 2, 3, 4)
    ortho_in, ortho_exp = ortho.reshape(2, experts, share, hidden)
    in_grad = in_grad.reshape(experts, share, hidden)
    exp_grad = exp_grad.reshape(experts, share, hidden)

    three_cols = 3 * head_cols
    last = gathered[n_t - 1, :width]
    packed_three = jnp.stack(
        [
            jnp.concatenate(
                [
                    gathered[b, :width, :three_cols],
                    last[:, b * head_cols : (b + 1) * head_cols],
                ],
                axis=1,
            )
            for b in range(3)
        ]
    )
    packed_out = jnp.concatenate([gathered[t, :width, three_cols:] for t in range(n_t)], axis=1)
    last_three, poly_three = ortho_call(packed_three)
    last_out, poly_out = ortho_call(packed_out[None])
    own_cols = jnp.where(
        t_index == n_t - 1,
        jnp.concatenate([last_three[b, :, three_cols:] for b in range(3)], axis=1),
        lax.dynamic_index_in_dim(last_three, jnp.minimum(t_index, 2), 0, False)[:, :three_cols],
    )
    own_rows = lax.dynamic_slice_in_dim(poly_three, d_index * share, share, 0)
    own_three = mm("ri,ic->rc", own_rows, own_cols)
    own_rows = lax.dynamic_slice_in_dim(poly_out, d_index * share, share, 0)
    own_cols = lax.dynamic_slice_in_dim(last_out[0], t_index * head_cols, head_cols, 1)
    own_out = mm("ri,ic->rc", own_rows, own_cols)
    own_qkv = own_three.reshape(share, 3, head_cols).transpose(1, 0, 2)
    qkv_new = w_qkv.astype(F32) - math.sqrt(3.0) * own_qkv
    attn_out_new = w_attn_out.astype(F32) - own_out.T

    norm_moment_new = DECAY * norm_moment + small[:4]
    norm_new = (
        jnp.concatenate([layer_norm_gains, layer_norm_biases], 0) - VEC_RATE * norm_moment_new
    )
    router_moment_turned = DECAY * m_router.T + small[4 : 4 + experts]
    router_moment_new = router_moment_turned.T
    router_new = w_router.astype(F32) - local_orthogonalize(router_moment_turned).T

    in_moment_new = DECAY * m_in + in_grad.astype(F32)
    exp_out_moment_new = DECAY * m_exp_out + jnp.swapaxes(exp_grad, 1, 2).astype(F32)
    in_new = w_in.astype(F32) - math.sqrt(max(1.0, FF / D)) * ortho_in.astype(F32)
    exp_out_new = w_exp_out.astype(F32) - jnp.swapaxes(ortho_exp, 1, 2).astype(F32)
    return (
        output,
        input_grad,
        norm_moment_new,
        norm_new,
        qkv_moment_new,
        qkv_new,
        attn_out_moment_new,
        attn_out_new,
        router_moment_new,
        router_new,
        in_moment_new,
        in_new,
        exp_out_moment_new,
        exp_out_new,
    )


def general(
    inputs,
    cotangent,
    expert_ids,
    layer_norm_gains,
    layer_norm_biases,
    norm_moment,
    w_qkv,
    w_attn_out,
    w_router,
    w_in,
    w_exp_out,
    m_qkv,
    m_attn_out,
    m_router,
    m_in,
    m_exp_out,
):
    rows, width = inputs.shape
    group_rows, top_count = expert_ids.shape
    experts, share, hidden = w_in.shape
    head_cols = w_attn_out.shape[0]
    heads = width // HD
    n_dp = lax.axis_size("dp")
    n_t = lax.axis_size("tensor")
    t_index = lax.axis_index("tensor")
    d_index = lax.axis_index("dp")
    per_host = max(1, experts // n_dp)
    copies = max(1, n_dp // experts)
    hosts = n_dp * per_host
    part = hidden // copies
    scale_qk = HD ** (-0.5)
    rows_pad = -(-rows // 16) * 16
    group_pad = n_t * rows_pad
    quarter = -(-(-(-CAP // n_t)) // 16) * 16
    slots = experts * quarter

    def padded(block):
        return jnp.pad(block, ((0, rows_pad - rows), (0, 0)))

    def group_of(block):
        return lax.all_gather(padded(block), "tensor", axis=0, tiled=True)

    def exchange(blocks, axis):
        return lax.all_to_all(blocks, axis, split_axis=0, concat_axis=0, tiled=True)

    def to_host(shard):
        parts = shard.reshape(experts, share, copies, part).transpose(0, 2, 1, 3)
        return exchange(parts.reshape(n_dp, per_host, share, part), "dp")

    def at_host(blocks):
        return blocks.transpose(1, 0, 2, 3).reshape(per_host, n_dp * share, part)

    def from_host(whole):
        blocks = whole.reshape(per_host, n_dp, share, part).transpose(1, 0, 2, 3)
        back = exchange(blocks, "dp").reshape(experts, copies, share, part)
        return back.transpose(0, 2, 1, 3).reshape(experts, share, copies * part)

    def pack_attention(three, out):
        return jnp.concatenate([three[0], three[1], three[2], out.T], axis=1)

    attn_weights = lax.all_gather(pack_attention(w_qkv, w_attn_out), "dp", axis=0, tiled=True)
    w_three, w_out_turned = attn_weights[:, : 3 * head_cols], attn_weights[:, 3 * head_cols :]
    w_exp_turned = jnp.swapaxes(w_exp_out, 1, 2)
    m_in_short = m_in.astype(BF)
    m_exp_short = jnp.swapaxes(m_exp_out.astype(BF), 1, 2)

    ids = expert_ids.reshape(n_t, rows, top_count)
    ids = jnp.pad(ids, ((0, 0), (0, rows_pad - rows), (0, 0)), constant_values=-1)
    ids = ids.reshape(group_pad, top_count)
    labels = lax.broadcasted_iota(jnp.int32, (group_pad, top_count, experts), 2)
    chosen = (ids[:, :, None] == labels).astype(F32)
    counted = jnp.sum(chosen, axis=1)
    earlier = (
        lax.broadcasted_iota(jnp.int32, (group_pad, group_pad), 0)
        > lax.broadcasted_iota(jnp.int32, (group_pad, group_pad), 1)
    ).astype(BF)
    before = mm("ts,se->te", earlier, counted.astype(BF))
    places = jnp.sum(before[:, None, :] * chosen, axis=2).astype(jnp.int32) - t_index * quarter
    mine = (places >= 0) & (places < quarter) & (ids >= 0)
    slot_of = jnp.where(mine, ids * quarter + places, -1)
    slot_rows = lax.broadcasted_iota(jnp.int32, (slots, group_pad), 0)
    picks = [slot_of[:, k][None, :] == slot_rows for k in range(top_count)]
    spread = sum(pick.astype(BF) for pick in picks)

    hidden_rows = inputs.astype(F32)
    first, first_normed, first_inverse = apply_layer_norm(
        hidden_rows, layer_norm_gains[0], layer_norm_biases[0]
    )
    act_one_group = group_of(first.astype(BF))
    cot_group = group_of(cotangent)
    images = rows // SEQ * n_t
    image_pad = group_pad // images

    def by_head(block):
        return block.reshape(images, image_pad, -1, HD)

    three = mm("td,dc->tc", act_one_group, w_three).astype(BF)
    query, key, value = [
        by_head(three[:, s * head_cols : (s + 1) * head_cols]) for s in range(3)
    ]
    scores = mm("bqhe,bkhe->bhqk", query, key) * scale_qk
    scores = jnp.where(lax.broadcasted_iota(jnp.int32, scores.shape, 3) < SEQ, scores, -1e30)
    expo = jnp.exp(scores - jnp.max(scores, axis=-1, keepdims=True))
    probs = expo / jnp.sum(expo, axis=-1, keepdims=True)
    probs_short = probs.astype(BF)
    mixed = mm("bhqk,bkhe->bqhe", probs_short, value).astype(BF).reshape(group_pad, head_cols)
    mixed = after(mixed, cot_group)
    attended = mm("te,de->td", mixed, w_out_turned).astype(BF)
    attended = lax.psum_scatter(attended, "tensor", scatter_dimension=0, tiled=True)
    middle = hidden_rows + attended[:rows].astype(F32)
    second, second_normed, second_inverse = apply_layer_norm(
        middle, layer_norm_gains[1], layer_norm_biases[1]
    )
    act_two = second.astype(BF)
    act_two_group = group_of(act_two)

    group_probs = jax.nn.softmax(mm("td,de->te", act_two_group, w_router), axis=-1)
    gates = jnp.sum(group_probs[:, None, :] * chosen, axis=2)
    gate_of_slot = sum(
        jnp.sum(jnp.where(pick, gates[:, k][None, :], 0.0), axis=1) for k, pick in enumerate(picks)
    )[:, None]
    slot_act = mm("st,td->sd", spread, act_two_group).astype(BF)
    cot_slot = mm("st,td->sd", spread, cot_group)
    slot_grad = (gate_of_slot * cot_slot).astype(BF)
    slot_pair = jnp.stack(
        [slot_act.reshape(experts, quarter, width), slot_grad.reshape(experts, quarter, width)], 1
    )
    if copies > 1:
        slot_pair = jnp.repeat(slot_pair, copies, axis=0)
    slot_pair = slot_pair.reshape(n_dp, per_host, 2, quarter, width)
    got = exchange(slot_pair, "dp")
    sent_in, sent_exp = to_host(w_in), to_host(w_exp_turned)
    sent_m_in, sent_m_exp = to_host(m_in_short), to_host(m_exp_short)
    host_in = at_host(sent_in)
    host_exp = at_host(sent_exp)
    in_grads, exp_grads, backs = [], [], []
    for e in range(per_host):
        e_rows, e_grad = [
            lax.all_gather(
                got[:, e, kind].reshape(n_dp * quarter, width), "tensor", axis=0, tiled=True
            )
            for kind in range(2)
        ]
        e_pre = mm("cd,df->cf", e_rows, host_in[e])
        normal = 0.5 * (1.0 + lax.erf(e_pre * INV_ROOT_TWO))
        slope = normal + e_pre * jnp.exp(-0.5 * e_pre * e_pre) * INV_ROOT_TWO_PI
        e_act = (e_pre * normal).astype(BF)
        e_grad_pre = (mm("cd,df->cf", e_grad, host_exp[e]) * slope).astype(BF)
        for part_sum in (
            mm("cf,df->cd", e_act, host_exp[e]),
            mm("cf,df->cd", e_grad_pre, host_in[e]),
        ):
            back = lax.psum_scatter(
                part_sum.astype(BF), "tensor", scatter_dimension=0, tiled=True
            )
            backs.append(back.reshape(n_dp, quarter, width))
        exp_grads.append(mm("cd,cf->df", e_grad, e_act))
        in_grads.append(mm("cd,cf->df", e_rows, e_grad_pre))
    host_in_grad, host_exp_grad = jnp.stack(in_grads), jnp.stack(exp_grads)

    back = jnp.stack(backs, axis=1)
    came = exchange(back, "dp").reshape(n_dp, per_host, 2, quarter, width)
    came = came.reshape(hosts // copies, copies, 2, quarter, width).astype(F32).sum(axis=1)
    moments = jnp.concatenate(
        [
            DECAY * at_host(sent_m_in).astype(F32) + host_in_grad,
            DECAY * at_host(sent_m_exp).astype(F32) + host_exp_grad,
        ],
        axis=0,
    ).astype(BF)
    in_grad = from_host(host_in_grad.astype(BF))
    exp_grad = from_host(host_exp_grad.astype(BF))
    members = [[e * copies + r for r in range(copies)] for e in range(n_dp // copies)]
    wide = lax.all_gather(moments, "tensor", axis=2, tiled=True)
    if copies > 1:
        wide = lax.all_gather(wide, "dp", axis=2, tiled=True, axis_index_groups=members)
    first_col = (lax.rem(d_index, copies) * n_t + t_index) * part
    own = [
        lax.dynamic_slice_in_dim(orthogonalize(wide[i]), first_col, part, 1)
        for i in range(2 * per_host)
    ]
    ortho = jnp.stack(own)

    slot_out = came[:, 0].reshape(slots, width)
    slot_row_grad = came[:, 1].reshape(slots, width).astype(BF)
    weighted = (gate_of_slot * slot_out).astype(BF)
    gate_grad_slot = jnp.sum(cot_slot * slot_out, axis=1)
    of_expert = (
        lax.broadcasted_iota(jnp.int32, (slots, 128), 0) // quarter
        == lax.broadcasted_iota(jnp.int32, (slots, 128), 1)
    )
    gate_grad_slot = jnp.where(of_expert, gate_grad_slot[:, None], 0.0).astype(BF)
    spread_cols = jnp.concatenate([weighted, slot_row_grad, gate_grad_slot], axis=1)
    token_part = mm("st,sc->tc", spread, spread_cols).astype(BF)
    token_sum = lax.psum_scatter(token_part, "tensor", scatter_dimension=0, tiled=True)
    token_sum = token_sum[:rows].astype(F32)
    output = (middle + token_sum[:, :width]).astype(BF)
    grad_probs = token_sum[:, 2 * width : 2 * width + experts]

    probs_local = jax.nn.softmax(mm("td,de->te", act_two, w_router), axis=-1)
    grad_logits = (
        probs_local * (grad_probs - jnp.sum(probs_local * grad_probs, axis=-1, keepdims=True))
    ).astype(BF)
    second_grad = token_sum[:, width : 2 * width] + mm("te,de->td", grad_logits, w_router)
    router_part = mm("td,te->ed", act_two, grad_logits)
    grad_mid_norm, gain_two_grad, bias_two_grad = norm_back(
        second_grad, second_normed, second_inverse, layer_norm_gains[1]
    )
    grad_middle = grad_mid_norm + cotangent.astype(F32)
    grad_mid_short = grad_middle.astype(BF)

    grad_mid_group = group_of(grad_mid_short)
    grad_heads = by_head(mm("td,de->te", grad_mid_group, w_out_turned).astype(BF))
    grad_weights = mm("bqhe,bkhe->bhqk", grad_heads, value)
    delta = jnp.sum(probs * grad_weights, axis=-1, keepdims=True)
    grad_scores = (probs * (grad_weights - delta)).astype(BF)
    grad_query = (mm("bhqk,bkhe->bqhe", grad_scores, key) * scale_qk).astype(BF)
    grad_key = (mm("bhqk,bqhe->bkhe", grad_scores, query) * scale_qk).astype(BF)
    grad_value = mm("bhqk,bqhe->bkhe", probs_short, grad_heads).astype(BF)
    grad_three = jnp.concatenate(
        [part.reshape(group_pad, head_cols) for part in (grad_query, grad_key, grad_value)], axis=1
    )
    first_grad = mm("tc,dc->td", grad_three, w_three).astype(BF)
    attn_grad = jnp.concatenate(
        [
            mm("td,tc->dc", act_one_group, grad_three).astype(BF),
            mm("td,tc->dc", grad_mid_group, mixed).astype(BF),
        ],
        axis=1,
    )
    attn_parts = exchange(attn_grad.reshape(n_dp, share, width), "dp")
    attn_sum = jnp.sum(attn_parts.astype(F32), axis=0)

    first_grad = lax.psum_scatter(first_grad, "tensor", scatter_dimension=0, tiled=True)
    grad_in_norm, gain_one_grad, bias_one_grad = norm_back(
        first_grad[:rows].astype(F32), first_normed, first_inverse, layer_norm_gains[0]
    )
    input_grad = grad_in_norm + grad_middle

    attn_moment = DECAY * pack_attention(m_qkv, m_attn_out) + attn_sum
    attn_blocks = attn_moment.reshape(share, 4, head_cols)
    qkv_moment_new = attn_blocks[:, :3].transpose(1, 0, 2)
    attn_out_moment_new = attn_blocks[:, 3].T
    vec_part = jnp.concatenate([gain_one_grad, gain_two_grad, bias_one_grad, bias_two_grad], 0)
    small_rows = -(-(4 + experts) // 8) * 8
    small_part = jnp.concatenate([vec_part, router_part], 0)
    small_part = jnp.pad(small_part, ((0, small_rows - 4 - experts), (0, 0)))
    gathered_dp = lax.all_gather(
        jnp.concatenate([attn_moment, small_part], 0).astype(BF), "dp", axis=0
    )
    small_part = jnp.sum(gathered_dp[:, share:].astype(F32), axis=0).astype(BF)
    gathered = jnp.concatenate([gathered_dp[:, :share].reshape(width, width), small_part], 0)
    gathered = lax.all_gather(gathered, "tensor", axis=0)
    small = jnp.sum(gathered[:, width:].astype(F32), axis=0)
    three_cols = 3 * head_cols
    last = gathered[n_t - 1, :width]
    packed_three = jnp.stack(
        [
            jnp.concatenate(
                [
                    gathered[b, :width, :three_cols],
                    last[:, b * head_cols : (b + 1) * head_cols],
                ],
                axis=1,
            )
            for b in range(3)
        ]
    )
    packed_out = jnp.concatenate([gathered[t, :width, three_cols:] for t in range(n_t)], axis=1)
    last_three, poly_three = ortho_call(packed_three)
    last_out, poly_out = ortho_call(packed_out[None])
    own_cols = jnp.where(
        t_index == n_t - 1,
        jnp.concatenate([last_three[b, :, three_cols:] for b in range(3)], axis=1),
        lax.dynamic_index_in_dim(last_three, jnp.minimum(t_index, 2), 0, False)[:, :three_cols],
    )
    own_rows = lax.dynamic_slice_in_dim(poly_three, d_index * share, share, 0)
    own_three = mm("ri,ic->rc", own_rows, own_cols)
    own_rows = lax.dynamic_slice_in_dim(poly_out, d_index * share, share, 0)
    own_cols = lax.dynamic_slice_in_dim(last_out[0], t_index * head_cols, head_cols, 1)
    own_out = mm("ri,ic->rc", own_rows, own_cols)
    own_qkv = own_three.reshape(share, 3, head_cols).transpose(1, 0, 2)
    qkv_new = w_qkv.astype(F32) - math.sqrt(3.0) * own_qkv
    attn_out_new = w_attn_out.astype(F32) - own_out.T

    norm_moment_new = DECAY * norm_moment + small[:4]
    norm_new = (
        jnp.concatenate([layer_norm_gains, layer_norm_biases], 0) - VEC_RATE * norm_moment_new
    )
    router_moment_turned = DECAY * m_router.T + small[4 : 4 + experts]
    router_moment_new = router_moment_turned.T
    router_new = w_router.astype(F32) - local_orthogonalize(router_moment_turned).T

    ortho_in, ortho_exp = from_host(ortho[:per_host]), from_host(ortho[per_host:])
    in_moment_new = DECAY * m_in + in_grad.astype(F32)
    exp_out_moment_new = DECAY * m_exp_out + jnp.swapaxes(exp_grad, 1, 2).astype(F32)
    in_new = w_in.astype(F32) - math.sqrt(max(1.0, FF / D)) * ortho_in.astype(F32)
    exp_out_new = w_exp_out.astype(F32) - jnp.swapaxes(ortho_exp, 1, 2).astype(F32)
    return (
        output,
        input_grad,
        norm_moment_new,
        norm_new,
        qkv_moment_new,
        qkv_new,
        attn_out_moment_new,
        attn_out_new,
        router_moment_new,
        router_new,
        in_moment_new,
        in_new,
        exp_out_moment_new,
        exp_out_new,
    )


def solution(mesh):
    both = P(("dp", "tensor"), None)
    cols = P(None, "dp", "tensor")
    turned = P(None, "tensor", "dp")
    in_specs = (
        both, both, P("dp", None), P(), P(), P(), cols, P("tensor", "dp"), P(), cols, turned,
        cols, P("tensor", "dp"), P(), cols, turned,
    )
    out_specs = (
        both, both, P(), P(), cols, cols, P("tensor", "dp"), P("tensor", "dp"), P(), P(),
        cols, cols, turned, turned,
    )
    n_dp, n_t = mesh.shape["dp"], mesh.shape["tensor"]
    whole = n_t == 4 and 2 * (EXPERTS // n_dp) == n_t and (D // n_dp) % 16 == 0
    step = local if whole else general
    return jax.shard_map(step, mesh=mesh, in_specs=in_specs, out_specs=out_specs, check_vma=False)
```

```python
import math

import jax
import jax.numpy as jnp
from jax import lax
from jax.experimental import pallas as pl
from jax.experimental.pallas import tpu as pltpu
from jax.sharding import PartitionSpec as P

D = 768
HD = 64
FF = 3072
CAP = 147
EXPERTS = 16
SEQ = 197

HIGH = lax.Precision.HIGHEST
LN_EPS = 1e-06
NS_EPS = 1e-07
NS_A = 3.4445
NS_B = -4.775
NS_C = 2.0315
DECAY = 0.5
VEC_RATE = 0.0002
INV_ROOT_TWO = 0.7071067811865476
INV_ROOT_TWO_PI = 0.3989422804014327
BF = jnp.bfloat16
F32 = jnp.float32


def mm(spec, left, right):
    return jnp.einsum(spec, left, right, preferred_element_type=F32)


def after(value, other):
    return lax.optimization_barrier((value, other))[0]


def apply_layer_norm(values, gain_row, offset_row):
    centre = values - jnp.mean(values, axis=-1, keepdims=True)
    inv_std = lax.rsqrt(jnp.mean(centre * centre, axis=-1, keepdims=True) + LN_EPS)
    normed = centre * inv_std
    return (normed * gain_row + offset_row, normed, inv_std)


def norm_back(grad_normed, normed, inv_std, gain_row):
    scaled = grad_normed * gain_row
    first_mean = jnp.mean(scaled, axis=-1, keepdims=True)
    second_mean = jnp.mean(scaled * normed, axis=-1, keepdims=True)
    grad_values = inv_std * (scaled - first_mean - normed * second_mean)
    gain_grad = jnp.sum(grad_normed * normed, axis=0, keepdims=True)
    return (grad_values, gain_grad, jnp.sum(grad_normed, axis=0, keepdims=True))


def local_orthogonalize(matrix):
    norm_value = jnp.sqrt(jnp.sum(matrix * matrix))
    current = matrix / (norm_value + NS_EPS)
    for repeat in range(5):
        square = jnp.dot(current, current.T, precision=HIGH)
        poly_term = NS_B * square + NS_C * jnp.dot(square, square, precision=HIGH)
        current = NS_A * current + jnp.dot(poly_term, current, precision=HIGH)
    return current


def orthogonalize(matrix):
    wide = matrix.astype(F32)
    inverse = 1.0 / (jnp.sqrt(jnp.sum(wide * wide)) + NS_EPS)
    rows = matrix.shape[0]
    unit = (
        lax.broadcasted_iota(jnp.int32, (rows, rows), 0)
        == lax.broadcasted_iota(jnp.int32, (rows, rows), 1)
    ).astype(F32)
    current = matrix
    for repeat in range(5):
        square = mm("ic,jc->ij", current, current)
        if repeat == 0:
            square = square * (inverse * inverse)
        rest = (square - unit).astype(BF)
        poly = (
            (NS_A - NS_C) * unit + (NS_B + 2.0 * NS_C) * square + NS_C * mm("ij,jk->ik", rest, rest)
        ).astype(BF)
        grown = mm("ij,jc->ic", poly, current)
        if repeat == 0:
            grown = grown * inverse
        current = grown.astype(BF)
    return current


def dot(left, right, left_dim, right_dim):
    return lax.dot_general(
        left, right, (((left_dim,), (right_dim,)), ((), ())), preferred_element_type=F32
    )


class Ortho:
    def __init__(self, current, square, rest, poly, size):
        self.current, self.square, self.rest, self.poly, self.size = (
            current, square, rest, poly, size
        )
        self.n = square.shape[0]
        self.blocks, self.w = current.shape[0], current.shape[-1]
        self.tile = 256
        self.cuts = [(i, i + self.tile) for i in range(0, self.n, self.tile)]

    def unit(self, first, last):
        shape = (last - first, self.n - first)
        return (
            lax.broadcasted_iota(jnp.int32, shape, 0) == lax.broadcasted_iota(jnp.int32, shape, 1)
        ).astype(F32)

    def clear(self):
        self.square[...] = jnp.zeros_like(self.square)

    def add_square(self, b):
        block = self.current[b].reshape(self.n, self.w)
        for first, last in self.cuts:
            self.square[first:last, first:] += dot(block[first:last, :], block[first:, :], 1, 1)

    def make_poly(self):
        square, rest, poly, cuts = self.square, self.rest, self.poly, self.cuts
        scale = self.size[...]
        scale_two = scale * scale
        for first, last in cuts:
            for low, high in cuts:
                if low > first:
                    square[low:high, first:last] = square[first:last, low:high].T
        for first, last in cuts:
            if first > 0:
                rest[first:last, :first] = (square[first:last, :first] * scale_two).astype(BF)
            rest[first:last, first:] = (
                square[first:last, first:] * scale_two - self.unit(first, last)
            ).astype(BF)
        for first, last in cuts:
            strip = scale * (
                (NS_A - NS_C) * self.unit(first, last)
                + (NS_B + 2.0 * NS_C) * scale_two * square[first:last, first:]
                + NS_C * dot(rest[first:last, :], rest[:, first:], 1, 0)
            )
            poly[first:last, first:] = strip.astype(BF)
            for low, high in cuts:
                if low > first:
                    poly[low:high, first:last] = strip[:, low - first : high - first].T.astype(BF)

    def measure(self):
        total = jnp.zeros((1, 1), F32)
        for first, last in self.cuts:
            diagonal = self.unit(first, last)[:, : self.tile] * self.square[first:last, first:last]
            total = total + jnp.sum(
                jnp.sum(diagonal, axis=1, keepdims=True), axis=0, keepdims=True
            )
        self.size[...] = 1.0 / (jnp.sqrt(total) + NS_EPS)

    def grown(self, b):
        block = self.current[b].reshape(self.n, self.w)
        return dot(self.poly[...], block, 1, 0).astype(BF)

    def steps(self):
        self.measure()

        @pl.loop(0, 4)
        def _(step):
            self.make_poly()
            self.size[...] = jnp.ones((1, 1), F32)
            self.clear()

            @pl.loop(0, self.blocks)
            def _(b):
                self.current[b] = self.grown(b).reshape(self.current.shape[1:])
                self.add_square(b)

        self.make_poly()


def ortho_kernel(x_ref, current, poly, square, rest, size):
    ortho = Ortho(current, square, rest, poly, size)
    ortho.clear()

    @pl.loop(0, ortho.blocks)
    def _(b):
        current[b] = x_ref[b]
        ortho.add_square(b)

    ortho.steps()


def ortho_call(blocks):
    count, n, w = blocks.shape
    vmem = pl.BlockSpec(memory_space=pltpu.VMEM)
    return pl.pallas_call(
        ortho_kernel,
        out_shape=(jax.ShapeDtypeStruct((count, n, w), BF), jax.ShapeDtypeStruct((n, n), BF)),
        in_specs=[vmem],
        out_specs=(vmem, vmem),
        scratch_shapes=[
            pltpu.VMEM((n, n), F32), pltpu.VMEM((n, n), BF), pltpu.VMEM((1, 1), F32)
        ],
        cost_estimate=pl.CostEstimate(
            flops=20 * count * n * n * w, bytes_accessed=4 * count * n * w, transcendentals=0
        ),
        compiler_params=pltpu.CompilerParams(vmem_limit_bytes=50 * 1024 * 1024),
        name="orthogonalize",
    )(blocks)


MESH = pl.DeviceIdType.MESH
PEERS = (4, 1, 5, 2, 6, 3, 7)


def experts_kernel(
    slots_ref, win_ref, wexp_ref,
    came_ref, gin_ref, gexp_ref,
    rows, weights, part, other, rows_of, hidden_of,
    tok_send, tok_recv, fwd_send, fwd_recv, sum_send, sum_recv, ret_send, ret_recv,
    wx_send, wx_recv, load_sem,
):
    n_experts, n_t, n_dp, pair, width = rows.shape
    quarter = pair // 2
    share = gin_ref.shape[2]
    d, t = lax.axis_index("dp"), lax.axis_index("tensor")
    sibling, across = (d, t ^ 1), (d, t ^ 2)
    count = n_dp * quarter

    def remote(source, target, send, recv, device):
        return pltpu.make_async_remote_copy(
            src_ref=source, dst_ref=target, send_sem=send, recv_sem=recv,
            device_id=device, device_id_type=MESH,
        )

    def tok(e, k):
        return remote(
            slots_ref.at[d ^ k, e], rows.at[e, 0, k],
            tok_send.at[e, k], tok_recv.at[e, k], (d ^ k, t),
        )

    def tok_own(e):
        return pltpu.make_async_copy(slots_ref.at[d, e], rows.at[e, 0, 0], tok_recv.at[e, 0])

    def forward(kind, e, k):
        source, target = ((0, 1), (0, 2), (2, 3))[kind]
        return remote(
            rows.at[e, source, k], rows.at[e, target, k],
            fwd_send.at[kind, e, k], fwd_recv.at[kind, e, k],
            across if kind == 1 else sibling,
        )

    def partial(stage, e):
        return remote(
            part.at[e, 3 - stage], other.at[e, stage],
            sum_send.at[stage, e], sum_recv.at[stage, e],
            across if stage == 1 else sibling,
        )

    def ret(e, k):
        return remote(
            part.at[e, 0, k], came_ref.at[d, e],
            ret_send.at[e, k], ret_recv.at[e, k], (d ^ k, t),
        )

    def ret_own(e):
        return pltpu.make_async_copy(part.at[e, 0, 0], came_ref.at[d, e], ret_recv.at[e, 0])

    def load(e):
        return pltpu.make_async_copy(win_ref.at[:, e], weights.at[0, e], load_sem.at[e])

    def second(e, k):
        return remote(
            wexp_ref.at[d ^ k, e], weights.at[1, e, d], wx_send.at[e, k], wx_recv.at[e, k], (d ^ k, t)
        )

    def second_own(e):
        return pltpu.make_async_copy(wexp_ref.at[d, e], weights.at[1, e, d], wx_recv.at[e, 0])

    def send(e):
        for k in PEERS:
            tok(e, k).start()
        for k in PEERS:
            second(e, k).start()

    def wait_second(e):
        second_own(e).wait()

        @pl.loop(1, n_dp)
        def _(k):
            second(e, k).wait_recv()

    barrier = pltpu.get_barrier_semaphore()

    @pl.loop(1, n_dp)
    def _(k):
        pl.semaphore_signal(barrier, inc=1, device_id=(d ^ k, t), device_id_type=MESH)

    pl.semaphore_signal(barrier, inc=1, device_id=sibling, device_id_type=MESH)
    pl.semaphore_signal(barrier, inc=1, device_id=across, device_id_type=MESH)
    for e in range(n_experts):
        tok_own(e).start()
        load(e).start()
        second_own(e).start()
    pl.semaphore_wait(barrier, n_dp + 1)
    send(0)

    def pass_on(e):
        for k in (0,) + PEERS:
            if k == 0:
                tok_own(e).wait()
            else:
                tok(e, k).wait_recv()
            forward(0, e, k).start()
            forward(1, e, k).start()

    def pass_again(e):
        for k in (0,) + PEERS:
            forward(1, e, k).wait_recv()
            forward(2, e, k).start()

        @pl.loop(0, n_dp)
        def _(k):
            forward(0, e, k).wait_recv()
            forward(2, e, k).wait_recv()

    def give_back(e):
        partial(1, e).wait_recv()
        partial(2, e).wait_recv()
        for k in range(n_dp):
            part[e, 0, k] = (
                part[e, 0, k].astype(F32) + other[e, 1, k].astype(F32) + other[e, 2, k].astype(F32)
            ).astype(BF)
        ret_own(e).start()
        for k in PEERS:
            ret(e, k).start()

    def weight_grads(e):
        gin_ref[:, e] = dot(rows_of[0], hidden_of[1], 0, 0).astype(BF).reshape(n_dp, share, width)
        gexp_ref[:, e] = dot(rows_of[1], hidden_of[0], 0, 0).astype(BF).reshape(n_dp, share, width)

    pass_on(0)
    pass_again(0)
    wait_second(0)
    send(1)
    for e in range(n_experts):
        load(e).wait()

    @pl.loop(0, n_experts * n_t)
    def _(step):
        e = step // n_t
        r = n_t - 1 - step % n_t
        w_in = weights[0, e].reshape(width, width)
        w_exp = weights[1, e].reshape(width, width)
        pairs = [rows[e, r, k].astype(F32) for k in range(n_dp)]
        act_rows = jnp.concatenate([block[:quarter] for block in pairs], axis=0).astype(BF)
        grad_rows = jnp.concatenate([block[quarter:] for block in pairs], axis=0).astype(BF)
        pre = dot(act_rows, w_in, 1, 0)
        normal = 0.5 * (1.0 + lax.erf(pre * INV_ROOT_TWO))
        slope = normal + pre * jnp.exp(-0.5 * pre * pre) * INV_ROOT_TWO_PI
        act = (pre * normal).astype(BF)
        grad_pre = (dot(grad_rows, w_exp, 1, 0) * slope).astype(BF)
        at = pl.ds(pl.multiple_of(r * count, count), count)
        rows_of[0, at] = act_rows
        rows_of[1, at] = grad_rows
        hidden_of[0, at] = act
        hidden_of[1, at] = grad_pre
        row_out, row_grad = dot(act, w_exp, 1, 1), dot(grad_pre, w_in, 1, 1)
        for k in range(n_dp):
            own = slice(k * quarter, (k + 1) * quarter)
            part[e, r, k] = jnp.concatenate([row_out[own], row_grad[own]], axis=0).astype(BF)

        @pl.when(r == n_t - 1)
        def _():
            partial(0, e).start()

        @pl.when(r == 2)
        def _():
            partial(0, e).wait_recv()
            for k in range(n_dp):
                part[e, 2, k] = (
                    part[e, 2, k].astype(F32) + other[e, 0, k].astype(F32)
                ).astype(BF)
            partial(1, e).start()

        @pl.when(r == 1)
        def _():
            partial(2, e).start()

        @pl.when(step == n_t - 1)
        def _():
            pass_on(1)
            weight_grads(0)
            pass_again(1)
            wait_second(1)
            give_back(0)

        @pl.when(step == 2 * n_t - 1)
        def _():
            weight_grads(1)
            give_back(1)

    for e in range(n_experts):
        ret_own(e).wait()
        for stage in range(3):
            partial(stage, e).wait_send()

        @pl.loop(0, n_dp)
        def _(k, e=e):
            for kind in range(3):
                forward(kind, e, k).wait_send()

        @pl.loop(1, n_dp)
        def _(k, e=e):
            tok(e, k).wait_send()
            second(e, k).wait_send()
            ret(e, k).wait_send()
            ret(e, k).wait_recv()


def experts_call(slots, w_in, w_exp):
    n_dp, n_experts, pair, width = slots.shape
    share = w_in.shape[2]
    n_t = lax.axis_size("tensor")
    anywhere = pl.BlockSpec(memory_space=pl.ANY)
    vmem = pl.BlockSpec(memory_space=pltpu.VMEM)
    grads = jax.ShapeDtypeStruct((n_dp, n_experts, share, width), BF)
    dma = pltpu.SemaphoreType.DMA
    part = (n_experts, n_t, n_dp, pair, width)
    rows = n_experts * n_t * n_dp * pair
    return pl.pallas_call(
        experts_kernel,
        out_shape=(jax.ShapeDtypeStruct(slots.shape, BF), grads, grads),
        in_specs=[anywhere] * 3,
        out_specs=(anywhere, vmem, vmem),
        scratch_shapes=[
            pltpu.VMEM(part, BF),
            pltpu.VMEM((2, n_experts, n_dp, share, width), BF),
            pltpu.VMEM(part, BF),
            pltpu.VMEM((n_experts, 3) + part[2:], BF),
            pltpu.VMEM((2, n_t * n_dp * pair // 2, width), BF),
            pltpu.VMEM((2, n_t * n_dp * pair // 2, width), BF),
            dma((n_experts, n_dp)),
            dma((n_experts, n_dp)),
            dma((3, n_experts, n_dp)),
            dma((3, n_experts, n_dp)),
            dma((3, n_experts)),
            dma((3, n_experts)),
            dma((n_experts, n_dp)),
            dma((n_experts, n_dp)),
            dma((n_experts, n_dp)),
            dma((n_experts, n_dp)),
            dma((n_experts,)),
        ],
        cost_estimate=pl.CostEstimate(
            flops=40 * rows * width * width, bytes_accessed=400_000_000, transcendentals=0
        ),
        compiler_params=pltpu.CompilerParams(
            collective_id=1, has_side_effects=True, vmem_limit_bytes=60 * 1024 * 1024
        ),
        name="experts",
    )(slots, w_in, w_exp)


def layer_norm_parts(values):
    centre = values - jnp.mean(values, axis=-1, keepdims=True)
    inv_std = lax.rsqrt(jnp.mean(centre * centre, axis=-1, keepdims=True) + LN_EPS)
    return centre * inv_std, inv_std


def remote(source, target, send, recv, device):
    return pltpu.make_async_remote_copy(
        src_ref=source, dst_ref=target, send_sem=send, recv_sem=recv,
        device_id=device, device_id_type=MESH,
    )


def greet(n_dp, d, t, more=0):
    barrier = pltpu.get_barrier_semaphore()

    @pl.loop(1, n_dp)
    def _(k):
        pl.semaphore_signal(barrier, inc=1, device_id=(d ^ k, t), device_id_type=MESH)

    pl.semaphore_signal(barrier, inc=1, device_id=(d, t ^ 1), device_id_type=MESH)
    pl.semaphore_signal(barrier, inc=1, device_id=(d, t ^ 2), device_id_type=MESH)
    pl.semaphore_wait(barrier, n_dp + 1 + more)


class Gather:
    def __init__(self, blocks, send, recv, d, t):
        self.copies = [
            remote(blocks.at[i], blocks.at[i], send.at[n], recv.at[n], (d, t ^ hop))
            for n, (i, hop) in enumerate(((t, 1), (t, 2), (t ^ 2, 1)))
        ]

    def start(self):
        self.copies[0].start()
        self.copies[1].start()

    def pass_on(self):
        self.copies[1].wait_recv()
        self.copies[2].start()

    def finish(self):
        self.copies[0].wait_recv()
        self.copies[2].wait_recv()

    def wait_sent(self):
        for copy in self.copies:
            copy.wait_send()


class Scatter:
    def __init__(self, block, landed, send, recv, d, t):
        self.block, self.landed = block, landed
        self.copies = [
            remote(block(3 - n), landed.at[n], send.at[n], recv.at[n], (d, t ^ hop))
            for n, hop in enumerate((1, 2, 1))
        ]

    def send(self, r):
        if r == 2:
            self.copies[0].wait_recv()
            own = self.block(2)
            own[...] = (own[...].astype(F32) + self.landed[0].astype(F32)).astype(BF)
        self.copies[3 - r].start()

    def total(self):
        self.copies[1].wait_recv()
        self.copies[2].wait_recv()
        return (
            self.block(0)[...].astype(F32)
            + self.landed[1].astype(F32)
            + self.landed[2].astype(F32)
        )

    def wait_sent(self):
        for copy in self.copies:
            copy.wait_send()


class Exchange:
    def __init__(self, blocks, target, send, recv, d, t):
        self.n_dp = blocks.shape[0]
        self.parts = (blocks, target, send, recv, d, t)

    def copy(self, k):
        blocks, target, send, recv, d, t = self.parts
        return remote(blocks.at[d ^ k], target.at[d], send.at[k], recv.at[k], (d ^ k, t))

    def own(self):
        blocks, target, send, recv, d, t = self.parts
        return pltpu.make_async_copy(blocks.at[d], target.at[d], recv.at[0])

    def start(self):
        self.own().start()
        for k in PEERS:
            self.copy(k).start()

    def finish(self):
        self.own().wait()

        @pl.loop(1, self.n_dp)
        def _(k):
            self.copy(k).wait_recv()

    def wait_sent(self):
        @pl.loop(1, self.n_dp)
        def _(k):
            self.copy(k).wait_send()


class Spread:
    def __init__(self, source, blocks, send, recv, d, t):
        self.own = pltpu.make_async_copy(source, blocks.at[d], recv.at[0])
        self.first = [
            remote(source, blocks.at[d], send.at[k], recv.at[k], (d ^ k, t)) for k in (1, 2, 4, 6)
        ]
        self.onward = [
            remote(blocks.at[d ^ k], blocks.at[d ^ k], send.at[k ^ 1], recv.at[k ^ 1], (d ^ 1, t))
            for k in (2, 4, 6)
        ]

    def start(self):
        self.own.start()
        for copy in (self.first[2], self.first[3], self.first[1], self.first[0]):
            copy.start()

    def finish(self):
        for n in range(3):
            self.first[n + 1].wait_recv()
            self.onward[n].start()
        self.own.wait()
        self.first[0].wait_recv()
        for copy in self.onward:
            copy.wait_recv()

    def wait_sent(self):
        for copy in self.first + self.onward:
            copy.wait_send()


def of_head(block, head):
    lane = lax.broadcasted_iota(jnp.int32, block.shape, 1)
    return jnp.where(lane // HD == head, block, jnp.zeros_like(block))


def head_probs(query, key, head):
    scores = dot(of_head(query, head), key, 1, 1) * HD ** (-0.5)
    seen = lax.broadcasted_iota(jnp.int32, scores.shape, 1) < SEQ
    scores = jnp.where(seen, scores, -1e30)
    expo = jnp.exp(scores - jnp.max(scores, axis=-1, keepdims=True))
    return expo / jnp.sum(expo, axis=-1, keepdims=True)


def only_tokens(block):
    row = lax.broadcasted_iota(jnp.int32, block.shape, 0)
    return jnp.where(row < SEQ, block, jnp.zeros_like(block))


def front_kernel(
    local_heads,
    x_ref, cot_ref, wp_ref, gains_ref, biases_ref, ids_ref, wr_ref, win_ref,
    a1_out, three_out, mixed_out, w_out, slots_out, middle_ref, cots_ref, gate_ref, slot_ref, win_out,
    a1, cot, a2, three, mixed, w, part, landed, slots,
    wt_send, wt_recv, in_send, in_recv,
    ag_send, ag_recv, sum_send, sum_recv, out_sem,
):
    n_dp, share, wide = w.shape
    n_t, rows, width = a1.shape
    third = width // 3
    d, t = lax.axis_index("dp"), lax.axis_index("tensor")
    greet(n_dp, d, t)

    weights = Spread(wp_ref, w, wt_send, wt_recv, d, t)
    weights.start()
    gathers = [Gather(ref, ag_send.at[n], ag_recv.at[n], d, t) for n, ref in enumerate((a1, cot, a2))]
    x = x_ref[...].astype(F32)
    normed, _ = layer_norm_parts(x)
    a1[t] = only_tokens(normed * gains_ref[0:1, :] + biases_ref[0:1, :]).astype(BF)
    cot[t] = cot_ref[...]
    gathers[0].start()
    gathers[1].start()
    gathers[0].pass_on()
    gathers[0].finish()
    weights.finish()
    bulk_in = Exchange(win_ref, win_out, in_send, in_recv, d, t)
    bulk_in.start()

    experts, quarter = wr_ref.shape[0], slots.shape[2] // 2
    label = lax.broadcasted_iota(jnp.int32, (experts, rows), 0)
    earlier = (
        lax.broadcasted_iota(jnp.int32, (rows, rows), 0)
        < lax.broadcasted_iota(jnp.int32, (rows, rows), 1)
    ).astype(BF)
    taken = jnp.zeros((experts, 1), F32)
    first_place = (t * quarter).astype(F32)
    chosen = []
    for image in range(n_t):
        named = [label == ids_ref[image, k : k + 1, :] for k in range(2)]
        chosen.append(named)
        counted = named[0].astype(F32) + named[1].astype(F32)
        before = taken + dot(counted.astype(BF), earlier, 1, 0)
        taken = taken + jnp.sum(counted, axis=1, keepdims=True)
        for k in range(2):
            place = jnp.sum(jnp.where(named[k], before, 0.0), axis=0, keepdims=True) - first_place
            ids = ids_ref[image, k : k + 1, :].astype(F32)
            mine = (place >= 0.0) & (place < quarter) & (ids >= 0.0)
            slot_ref[image, k : k + 1, :] = jnp.where(mine, ids * quarter + place, -1.0)

    sums = Scatter(lambda r: part.at[r], landed, sum_send, sum_recv, d, t)
    for r in reversed(range(n_t)):
        image = t ^ r
        every = w[...].reshape(n_dp * share, wide)
        qkv = dot(a1[image], every[:, :width], 1, 0).astype(BF)
        three[image] = qkv
        query, key, value = [qkv[:, s * third : (s + 1) * third] for s in range(3)]
        heads = jnp.zeros((rows, third), F32)
        for head in range(local_heads):
            probs = head_probs(query, key, head).astype(BF)
            heads = heads + dot(probs, of_head(value, head), 1, 0)
        mixed[image] = heads.astype(BF)
        part[r] = dot(mixed[image], every[:, width:], 1, 1).astype(BF)
        if r > 0:
            sums.send(r)
        if r == 1:
            gathers[1].pass_on()
    middle = x + only_tokens(sums.total())
    middle_ref[...] = middle
    normed, _ = layer_norm_parts(middle)
    a2[t] = only_tokens(normed * gains_ref[1:2, :] + biases_ref[1:2, :]).astype(BF)
    gathers[2].start()
    outs = [
        pltpu.make_async_copy(source, target, out_sem.at[n])
        for n, (source, target) in enumerate(
            ((a1, a1_out), (three, three_out), (mixed, mixed_out), (w, w_out), (slots, slots_out))
        )
    ]
    for out in outs[:4]:
        out.start()
    gathers[1].finish()
    gathers[2].pass_on()
    gathers[2].finish()

    gates = []
    for image in range(n_t):
        logits = dot(wr_ref[...], a2[image], 1, 1)
        expo = jnp.exp(logits - jnp.max(logits, axis=0, keepdims=True))
        probs = expo / jnp.sum(expo, axis=0, keepdims=True)
        gates.append(
            [jnp.sum(jnp.where(chosen[image][k], probs, 0.0), axis=0, keepdims=True) for k in range(2)]
        )
    pairs = slots.shape[1]
    held = pairs * quarter

    @pl.loop(0, n_dp)
    def _(host):
        number = lax.broadcasted_iota(jnp.int32, (held, rows), 0) + host * held
        number = number.astype(F32)
        slot_act = jnp.zeros((held, width), F32)
        slot_cot = jnp.zeros((held, width), F32)
        gate = jnp.zeros((held, 1), F32)
        for image in range(n_t):
            picks = [slot_ref[image, k : k + 1, :] == number for k in range(2)]
            spread = jnp.where(picks[0] | picks[1], 1.0, 0.0).astype(BF)
            slot_act = slot_act + dot(spread, a2[image], 1, 0)
            slot_cot = slot_cot + dot(spread, cot[image], 1, 0)
            for k in range(2):
                gate = gate + jnp.sum(
                    jnp.where(picks[k], gates[image][k], 0.0), axis=1, keepdims=True
                )
        slot_grad = gate * slot_cot
        gate_ref[host] = gate
        cots_ref[host] = slot_cot.astype(BF)
        for e in range(pairs):
            own = slice(e * quarter, (e + 1) * quarter)
            slots[host, e] = jnp.concatenate([slot_act[own], slot_grad[own]], axis=0).astype(BF)

    outs[4].start()
    for out in outs:
        out.wait()
    weights.wait_sent()
    sums.wait_sent()
    for gather in gathers:
        gather.wait_sent()
    bulk_in.finish()
    bulk_in.wait_sent()


def front_call(x, cot, wp, gains, biases, ids, w_router, w_in, quarter, local_heads):
    n_dp, n_t = w_in.shape[0], lax.axis_size("tensor")
    rows, width = x.shape
    share, wide = wp.shape
    anywhere = pl.BlockSpec(memory_space=pl.ANY)
    vmem = pl.BlockSpec(memory_space=pltpu.VMEM)
    dma = pltpu.SemaphoreType.DMA

    def shape(*dims, kind=BF):
        return jax.ShapeDtypeStruct(dims, kind)

    group = (n_t, rows, width)
    pairs = w_in.shape[1]
    slots = (n_dp, pairs, 2 * quarter, width)
    return pl.pallas_call(
        lambda *refs: front_kernel(local_heads, *refs),
        out_shape=(
            shape(*group), shape(*group), shape(n_t, rows, width // 3), shape(n_dp, share, wide),
            shape(*slots), shape(rows, width, kind=F32), shape(n_dp, pairs * quarter, width),
            shape(n_dp, pairs * quarter, 1, kind=F32), shape(n_t, 2, rows, kind=F32),
            shape(*w_in.shape),
        ),
        in_specs=[vmem, vmem, anywhere, vmem, vmem, vmem, vmem, anywhere],
        out_specs=(anywhere,) * 5 + (vmem,) * 4 + (anywhere,),
        scratch_shapes=[pltpu.VMEM(group, BF)] * 4
        + [
            pltpu.VMEM((n_t, rows, width // 3), BF),
            pltpu.VMEM((n_dp, share, wide), BF),
            pltpu.VMEM(group, BF),
            pltpu.VMEM((n_t - 1, rows, width), BF),
            pltpu.VMEM(slots, BF),
        ]
        + [dma((n_dp,))] * 4
        + [dma((3, 3)), dma((3, 3)), dma((3,)), dma((3,)), dma((5,))],
        cost_estimate=pl.CostEstimate(
            flops=4 * n_t * rows * width * wide, bytes_accessed=400_000_000, transcendentals=0
        ),
        compiler_params=pltpu.CompilerParams(
            collective_id=2, has_side_effects=True, vmem_limit_bytes=50 * 1024 * 1024
        ),
        name="front",
    )(x, cot, wp, gains, biases, ids, w_router, w_in)


def back_kernel(
    local_heads, experts,
    came_ref, cots_ref, gate_ref, slot_ref, middle_ref, x_ref, cot_ref, gains_ref, biases_ref, wr_ref,
    a1_ref, three_ref, mixed_ref, w_ref, min_ref, mexp_ref, gin_ref, gexp_ref,
    output_ref, input_grad_ref, attn_ref, small_ref, min_out, mexp_out, gin_out, gexp_out,
    tok, cols, tok_landed, gm, part, landed, grads, sum_three, sum_out, shares,
    in_send, in_recv, exp_send, exp_recv, at_send, at_recv,
    ag_send, ag_recv, tok_send, tok_recv, sum_send, sum_recv,
):
    n_dp, share, wide = w_ref.shape
    n_t, rows, width = a1_ref.shape
    third = width // 3
    d, t = lax.axis_index("dp"), lax.axis_index("tensor")
    greet(n_dp, d, t)
    bulks = [
        Exchange(min_ref, min_out, in_send, in_recv, d, t),
        Exchange(mexp_ref, mexp_out, exp_send, exp_recv, d, t),
    ]
    for bulk in bulks:
        bulk.start()

    pairs, quarter = came_ref.shape[1], came_ref.shape[2] // 2
    held = pairs * quarter

    @pl.loop(0, n_dp)
    def _(host):
        at = pl.ds(pl.multiple_of(host * held, held), held)
        came = [came_ref[host, e].astype(F32) for e in range(pairs)]
        slot_out = jnp.concatenate([block[:quarter] for block in came], axis=0)
        row_grad = jnp.concatenate([block[quarter:] for block in came], axis=0)
        gate_grad = jnp.sum(cots_ref[host].astype(F32) * slot_out, axis=1, keepdims=True)
        lane = lax.broadcasted_iota(jnp.int32, (held, 128), 1) - host * pairs
        row = lax.broadcasted_iota(jnp.int32, (held, 128), 0)
        named = (row >= lane * quarter) & (row < (lane + 1) * quarter)
        cols[at, :width] = (gate_ref[host] * slot_out).astype(BF)
        cols[at, width : 2 * width] = row_grad.astype(BF)
        cols[at, 2 * width :] = jnp.where(
            named, jnp.broadcast_to(gate_grad, named.shape), 0.0
        ).astype(BF)

    tokens = Scatter(lambda r: tok.at[t ^ r], tok_landed, tok_send, tok_recv, d, t)
    number = lax.broadcasted_iota(jnp.int32, (cols.shape[0], rows), 0).astype(F32)
    for r in reversed(range(n_t)):
        image = t ^ r
        picks = [slot_ref[image, k : k + 1, :] == number for k in range(2)]
        spread = jnp.where(picks[0] | picks[1], 1.0, 0.0).astype(BF)
        tok[image] = dot(spread, cols[...], 0, 0).astype(BF)
        if r > 0:
            tokens.send(r)
    middle = middle_ref[...]
    gain_two = gains_ref[1:2, :]
    normed_two, inverse_two = layer_norm_parts(middle)
    act_two = only_tokens(normed_two * gain_two + biases_ref[1:2, :]).astype(BF)
    logits = dot(act_two, wr_ref[...], 1, 0)
    logits = jnp.where(lax.broadcasted_iota(jnp.int32, logits.shape, 1) < experts, logits, -1e30)
    expo = jnp.exp(logits - jnp.max(logits, axis=-1, keepdims=True))
    probs = expo / jnp.sum(expo, axis=-1, keepdims=True)
    total = tokens.total()
    output_ref[...] = (middle + total[:, :width]).astype(BF)
    grad_probs = total[:, 2 * width :]
    grad_logits = probs * (grad_probs - jnp.sum(probs * grad_probs, axis=-1, keepdims=True))
    grad_logits = only_tokens(grad_logits).astype(BF)
    second_grad = only_tokens(total[:, width : 2 * width]) + dot(grad_logits, wr_ref[...], 1, 1)
    grad_middle, gain_two_grad, bias_two_grad = norm_back(
        second_grad, normed_two, inverse_two, gain_two
    )
    grad_middle = only_tokens(grad_middle + cot_ref[...].astype(F32))
    input_grad_ref[...] = grad_middle
    gm[t] = grad_middle.astype(BF)
    gather = Gather(gm, ag_send, ag_recv, d, t)
    gather.start()
    small_ref[...] = jnp.zeros_like(small_ref)
    small_ref[1:2, :] = gain_two_grad
    small_ref[3:4, :] = bias_two_grad
    small_ref[4 : 4 + experts, :] = dot(grad_logits, act_two, 0, 0)[:experts]
    sum_three[...] = jnp.zeros_like(sum_three)
    sum_out[...] = jnp.zeros_like(sum_out)
    gather.pass_on()
    gather.finish()

    sums = Scatter(lambda r: part.at[r], landed, sum_send, sum_recv, d, t)
    for r in reversed(range(n_t)):
        image = t ^ r
        every = w_ref[...].reshape(n_dp * share, wide)
        grad_rows = gm[image]
        qkv = three_ref[image]
        query, key, value = [qkv[:, s * third : (s + 1) * third] for s in range(3)]
        grad_mixed = dot(grad_rows, every[:, width:], 1, 0).astype(BF)
        grad_query = jnp.zeros((rows, third), F32)
        grad_key = jnp.zeros((rows, third), F32)
        grad_value = jnp.zeros((rows, third), F32)
        for head in range(local_heads):
            head_weights = head_probs(query, key, head)
            grad_head = of_head(grad_mixed, head)
            grad_weights = dot(grad_head, value, 1, 1)
            delta = jnp.sum(head_weights * grad_weights, axis=-1, keepdims=True)
            grad_scores = (head_weights * (grad_weights - delta)).astype(BF)
            grad_query = grad_query + dot(grad_scores, of_head(key, head), 1, 0)
            grad_key = grad_key + dot(grad_scores, of_head(query, head), 0, 0)
            grad_value = grad_value + dot(head_weights.astype(BF), grad_head, 0, 0)
        grad_three = jnp.concatenate(
            [
                (grad_query * HD ** (-0.5)).astype(BF),
                (grad_key * HD ** (-0.5)).astype(BF),
                grad_value.astype(BF),
            ],
            axis=1,
        )
        part[r] = dot(grad_three, every[:, :width], 1, 1).astype(BF)
        if r > 0:
            sums.send(r)
        sum_three[...] += dot(a1_ref[image], grad_three, 0, 0)
        sum_out[...] += dot(grad_rows, mixed_ref[image], 0, 0)
    grads[:, :, :width] = sum_three[...].astype(BF).reshape(n_dp, share, width)
    grads[:, :, width:] = sum_out[...].astype(BF).reshape(n_dp, share, third)
    over_y = [
        remote(
            grads.at[d ^ 1 ^ (2 * i)], shares.at[i], at_send.at[i], at_recv.at[i], (d ^ 1, t)
        )
        for i in range(4)
    ]
    along_z = [
        remote(
            shares.at[i], shares.at[4 + i], at_send.at[4 + i], at_recv.at[4 + i], (d ^ (2 * i), t)
        )
        for i in range(1, 4)
    ]
    for copy in over_y:
        copy.start()

    for i in (2, 3, 1, 0):
        over_y[i].wait_recv()
        shares[i] = (shares[i].astype(F32) + grads[d ^ (2 * i)].astype(F32)).astype(BF)
        if i > 0:
            along_z[i - 1].start()

    first_grad = only_tokens(sums.total())
    normed_one, inverse_one = layer_norm_parts(x_ref[...].astype(F32))
    grad_in, gain_one_grad, bias_one_grad = norm_back(
        first_grad, normed_one, inverse_one, gains_ref[0:1, :]
    )
    input_grad_ref[...] += grad_in
    small_ref[0:1, :] = gain_one_grad
    small_ref[2:3, :] = bias_one_grad
    total = shares[0].astype(F32)
    for i in range(1, 4):
        along_z[i - 1].wait_recv()
        total = total + shares[4 + i].astype(F32)
    attn_ref[...] = total
    for copy in over_y + along_z:
        copy.wait_send()
    gather.wait_sent()
    tokens.wait_sent()
    sums.wait_sent()
    for bulk in bulks:
        bulk.finish()
        bulk.wait_sent()


def back_call(
    came, cots, gate, slot, middle, x, cot, gains, biases, w_router, a1, three, mixed, w,
    m_in, m_exp, g_in, g_exp, local_heads, experts,
):
    n_dp, share, wide = w.shape
    n_t, rows, width = a1.shape
    anywhere = pl.BlockSpec(memory_space=pl.ANY)
    vmem = pl.BlockSpec(memory_space=pltpu.VMEM)
    dma = pltpu.SemaphoreType.DMA
    small_rows = -(-(4 + experts) // 8) * 8
    cols = 2 * width + 128
    return pl.pallas_call(
        lambda *refs: back_kernel(local_heads, experts, *refs),
        out_shape=(
            jax.ShapeDtypeStruct((rows, width), BF),
            jax.ShapeDtypeStruct((rows, width), F32),
            jax.ShapeDtypeStruct((share, wide), F32),
            jax.ShapeDtypeStruct((small_rows, width), F32),
        )
        + (jax.ShapeDtypeStruct(m_exp.shape, BF),) * 4,
        in_specs=[vmem] * 14 + [anywhere] * 4,
        out_specs=(vmem,) * 4 + (anywhere,) * 4,
        input_output_aliases={16: 6, 17: 7},
        scratch_shapes=[
            pltpu.VMEM((n_t, rows, cols), BF),
            pltpu.VMEM((experts * came.shape[2] // 2, cols), BF),
            pltpu.VMEM((n_t - 1, rows, cols), BF),
            pltpu.VMEM((n_t, rows, width), BF),
            pltpu.VMEM((n_t, rows, width), BF),
            pltpu.VMEM((n_t - 1, rows, width), BF),
            pltpu.VMEM((n_dp, share, wide), BF),
            pltpu.VMEM((width, width), F32),
            pltpu.VMEM((width, width // 3), F32),
            pltpu.VMEM((n_dp, share, wide), BF),
        ]
        + [dma((n_dp,))] * 6
        + [dma((3,))] * 6,
        cost_estimate=pl.CostEstimate(
            flops=20 * n_t * rows * width * wide, bytes_accessed=300_000_000, transcendentals=0
        ),
        compiler_params=pltpu.CompilerParams(
            collective_id=3, has_side_effects=True, vmem_limit_bytes=56 * 1024 * 1024
        ),
        name="back",
    )(
        came, cots, gate, slot, middle, x, cot, gains, biases, w_router, a1, three, mixed, w,
        m_in, m_exp, g_in, g_exp,
    )


def last_kernel(
    min_ref, mexp_ref, gin_ref, gexp_ref, pay_ref,
    ortho_ref, gin_out, gexp_out, all_out, small_ref,
    held, grown, moments, current, pays, alls, square, rest, poly, size,
    load_sem, pay_send, pay_recv, in_send, in_recv, exp_send, exp_recv,
    mat_send, mat_recv, ag_send, ag_recv, out_sem,
):
    n_dp, n_experts, share, width = gin_ref.shape
    n_t = moments.shape[0]
    d, t = lax.axis_index("dp"), lax.axis_index("tensor")
    loads = []
    for q in range(n_t):
        kind, e = divmod(q, n_experts)
        for n, (source, target) in enumerate(
            (((min_ref, mexp_ref)[kind], held), ((gin_ref, gexp_ref)[kind], grown))
        ):
            loads.append(
                pltpu.make_async_copy(source.at[:, e], target.at[q], load_sem.at[n, q])
            )
    for load in loads:
        load.start()
    barrier = pltpu.get_barrier_semaphore()
    pl.semaphore_signal(barrier, inc=1, device_id=(d, t ^ 3), device_id_type=MESH)
    greet(n_dp, d, t, 1)

    pay = Spread(pay_ref, pays, pay_send, pay_recv, d, t)
    pay.start()
    bulks = [
        Exchange(gin_ref, gin_out, in_send, in_recv, d, t),
        Exchange(gexp_ref, gexp_out, exp_send, exp_recv, d, t),
    ]
    for bulk in bulks:
        bulk.start()
    for load in loads:
        load.wait()

    @pl.loop(0, n_t)
    def _(q):
        for k in range(n_dp):
            moments[q, k] = (DECAY * held[q, k].astype(F32) + grown[q, k].astype(F32)).astype(BF)

    def matrix(step):
        return remote(
            moments.at[t ^ step], current.at[step],
            mat_send.at[step], mat_recv.at[step], (d, t ^ step),
        )

    own_matrix = pltpu.make_async_copy(moments.at[t], current.at[0], mat_recv.at[0])
    own_matrix.start()
    for step in (2, 3, 1):
        matrix(step).start()

    pay.finish()
    total = jnp.zeros((pays.shape[1] - share, width), F32)
    for k in range(n_dp):
        alls[t, k * share : (k + 1) * share] = pays[k, :share]
        total = total + pays[k, share:].astype(F32)
    alls[t, n_dp * share :] = total.astype(BF)
    gather = Gather(alls, ag_send, ag_recv, d, t)

    ortho = Ortho(current, square, rest, poly, size)
    ortho.clear()
    own_matrix.wait()
    ortho.add_square(0)
    matrix(1).wait_recv()
    ortho.add_square(1)
    gather.start()
    for step in (2, 3):
        matrix(step).wait_recv()
        ortho.add_square(step)
    ortho.steps()
    gather.pass_on()
    for b in range(n_t):
        block = ortho.grown(b)
        for k in range(n_dp):
            ortho_ref[k, t ^ b] = block[k * share : (k + 1) * share]
    gather.finish()
    out = pltpu.make_async_copy(alls, all_out, out_sem)
    out.start()
    small = jnp.zeros(small_ref.shape, F32)
    for b in range(n_t):
        small = small + alls[b, n_dp * share :].astype(F32)
    small_ref[...] = small
    out.wait()
    gather.wait_sent()
    for step in range(1, n_t):
        matrix(step).wait_send()

    pay.wait_sent()
    for bulk in bulks:
        bulk.finish()
        bulk.wait_sent()


def last_call(m_in, m_exp, g_in, g_exp, pay):
    n_dp, n_experts, share, width = g_in.shape
    n_t = lax.axis_size("tensor")
    anywhere = pl.BlockSpec(memory_space=pl.ANY)
    vmem = pl.BlockSpec(memory_space=pltpu.VMEM)
    dma = pltpu.SemaphoreType.DMA
    mats = pltpu.VMEM((n_t, n_dp, share, width), BF)
    every = (n_t, n_dp * share + pay.shape[0] - share, width)
    bulk = jax.ShapeDtypeStruct(g_in.shape, BF)
    return pl.pallas_call(
        last_kernel,
        out_shape=(
            jax.ShapeDtypeStruct((n_dp, n_t, share, width), BF),
            bulk,
            bulk,
            jax.ShapeDtypeStruct(every, BF),
            jax.ShapeDtypeStruct((pay.shape[0] - share, width), F32),
        ),
        in_specs=[anywhere] * 5,
        out_specs=(vmem, anywhere, anywhere, anywhere, vmem),
        scratch_shapes=[
            mats,
            mats,
            mats,
            mats,
            pltpu.VMEM((n_dp,) + pay.shape, BF),
            pltpu.VMEM(every, BF),
            pltpu.VMEM((width, width), F32),
            pltpu.VMEM((width, width), BF),
            pltpu.VMEM((width, width), BF),
            pltpu.VMEM((1, 1), F32),
            dma((2, n_t)),
        ]
        + [dma((n_dp,))] * 6
        + [dma((n_t,))] * 2
        + [dma((3,))] * 2
        + [dma],
        cost_estimate=pl.CostEstimate(
            flops=80 * width * width * width, bytes_accessed=300_000_000, transcendentals=0
        ),
        compiler_params=pltpu.CompilerParams(
            collective_id=4, has_side_effects=True, vmem_limit_bytes=58 * 1024 * 1024
        ),
        name="last",
    )(m_in, m_exp, g_in, g_exp, pay)


def local(
    inputs,
    cotangent,
    expert_ids,
    layer_norm_gains,
    layer_norm_biases,
    norm_moment,
    w_qkv,
    w_attn_out,
    w_router,
    w_in,
    w_exp_out,
    m_qkv,
    m_attn_out,
    m_router,
    m_in,
    m_exp_out,
):
    rows, width = inputs.shape
    group_rows, top_count = expert_ids.shape
    experts, share, hidden = w_in.shape
    head_cols = w_attn_out.shape[0]
    n_dp = lax.axis_size("dp")
    n_t = lax.axis_size("tensor")
    t_index = lax.axis_index("tensor")
    d_index = lax.axis_index("dp")
    per_host = experts // n_dp
    rows_pad = -(-rows // 16) * 16
    quarter = -(-(-(-CAP // n_t)) // 8) * 8
    third = width // 3

    def padded(block):
        return jnp.pad(block, ((0, rows_pad - rows), (0, 0)))

    def by_host(shard):
        return shard.reshape(n_dp, per_host, share, hidden)

    def pack_attention(three, out):
        return jnp.concatenate([three[0], three[1], three[2], out.T], axis=1)

    blocks = pack_attention(w_qkv, w_attn_out).reshape(share, 4, head_cols)
    blocks = jnp.pad(blocks, ((0, 0), (0, 0), (0, third - head_cols))).reshape(share, 4 * third)
    x_pad, cot_pad = padded(inputs), padded(cotangent)
    ids = jnp.pad(
        expert_ids.reshape(n_t, rows, top_count).transpose(0, 2, 1),
        ((0, 0), (0, 0), (0, rows_pad - rows)),
        constant_values=-1,
    )
    act_one_group, three, mixed, attn_weights, slot_pair, middle, cots, gate, slot, sent_in = front_call(
        x_pad,
        cot_pad,
        blocks,
        layer_norm_gains,
        layer_norm_biases,
        ids,
        w_router.T,
        by_host(w_in),
        quarter,
        head_cols // HD,
    )
    came, in_grad_parts, exp_grad_parts = experts_call(
        slot_pair, sent_in, by_host(jnp.swapaxes(w_exp_out, 1, 2))
    )

    results = back_call(
        came,
        cots,
        gate,
        slot,
        middle,
        x_pad,
        cot_pad,
        layer_norm_gains,
        layer_norm_biases,
        jnp.pad(w_router, ((0, 0), (0, 128 - experts))),
        act_one_group,
        three,
        mixed,
        attn_weights,
        by_host(m_in.astype(BF)),
        by_host(jnp.swapaxes(m_exp_out.astype(BF), 1, 2)),
        in_grad_parts,
        exp_grad_parts,
        head_cols // HD,
        experts,
    )
    output, input_grad, attn_sum, small_part = results[:4]
    sent_m_in, sent_m_exp, in_grad_parts, exp_grad_parts = results[4:]
    output, input_grad = output[:rows], input_grad[:rows]
    attn_sum = attn_sum.reshape(share, 4, third)[:, :, :head_cols].reshape(share, width)

    attn_moment = DECAY * pack_attention(m_qkv, m_attn_out) + attn_sum
    attn_blocks = attn_moment.reshape(share, 4, head_cols)
    qkv_moment_new = attn_blocks[:, :3].transpose(1, 0, 2)
    attn_out_moment_new = attn_blocks[:, 3].T
    pay_rows = -(-small_part.shape[0] // 16) * 16
    small_part = jnp.pad(small_part, ((0, pay_rows - small_part.shape[0]), (0, 0)))
    pay = jnp.concatenate([attn_moment, small_part], 0).astype(BF)

    ortho, in_grad, exp_grad, gathered, small = last_call(
        sent_m_in, sent_m_exp, in_grad_parts, exp_grad_parts, pay
    )
    ortho = lax.all_to_all(
        ortho.reshape(n_dp * n_t, share, hidden),
        ("dp", "tensor"),
        split_axis=0,
        concat_axis=0,
        tiled=True,
    )
    ortho = ortho.reshape(n_dp, 2, per_host, share, hidden).transpose(1, 0, 2, 3, 4)
    ortho_in, ortho_exp = ortho.reshape(2, experts, share, hidden)
    in_grad = in_grad.reshape(experts, share, hidden)
    exp_grad = exp_grad.reshape(experts, share, hidden)

    three_cols = 3 * head_cols
    last = gathered[n_t - 1, :width]
    packed_three = jnp.stack(
        [
            jnp.concatenate(
                [
                    gathered[b, :width, :three_cols],
                    last[:, b * head_cols : (b + 1) * head_cols],
                ],
                axis=1,
            )
            for b in range(3)
        ]
    )
    packed_out = jnp.concatenate([gathered[t, :width, three_cols:] for t in range(n_t)], axis=1)
    last_three, poly_three = ortho_call(packed_three)
    last_out, poly_out = ortho_call(packed_out[None])
    own_cols = jnp.where(
        t_index == n_t - 1,
        jnp.concatenate([last_three[b, :, three_cols:] for b in range(3)], axis=1),
        lax.dynamic_index_in_dim(last_three, jnp.minimum(t_index, 2), 0, False)[:, :three_cols],
    )
    own_rows = lax.dynamic_slice_in_dim(poly_three, d_index * share, share, 0)
    own_three = mm("ri,ic->rc", own_rows, own_cols)
    own_rows = lax.dynamic_slice_in_dim(poly_out, d_index * share, share, 0)
    own_cols = lax.dynamic_slice_in_dim(last_out[0], t_index * head_cols, head_cols, 1)
    own_out = mm("ri,ic->rc", own_rows, own_cols)
    own_qkv = own_three.reshape(share, 3, head_cols).transpose(1, 0, 2)
    qkv_new = w_qkv.astype(F32) - math.sqrt(3.0) * own_qkv
    attn_out_new = w_attn_out.astype(F32) - own_out.T

    norm_moment_new = DECAY * norm_moment + small[:4]
    norm_new = (
        jnp.concatenate([layer_norm_gains, layer_norm_biases], 0) - VEC_RATE * norm_moment_new
    )
    router_moment_turned = DECAY * m_router.T + small[4 : 4 + experts]
    router_moment_new = router_moment_turned.T
    router_new = w_router.astype(F32) - local_orthogonalize(router_moment_turned).T

    in_moment_new = DECAY * m_in + in_grad.astype(F32)
    exp_out_moment_new = DECAY * m_exp_out + jnp.swapaxes(exp_grad, 1, 2).astype(F32)
    in_new = w_in.astype(F32) - math.sqrt(max(1.0, FF / D)) * ortho_in.astype(F32)
    exp_out_new = w_exp_out.astype(F32) - jnp.swapaxes(ortho_exp, 1, 2).astype(F32)
    return (
        output,
        input_grad,
        norm_moment_new,
        norm_new,
        qkv_moment_new,
        qkv_new,
        attn_out_moment_new,
        attn_out_new,
        router_moment_new,
        router_new,
        in_moment_new,
        in_new,
        exp_out_moment_new,
        exp_out_new,
    )


def general(
    inputs,
    cotangent,
    expert_ids,
    layer_norm_gains,
    layer_norm_biases,
    norm_moment,
    w_qkv,
    w_attn_out,
    w_router,
    w_in,
    w_exp_out,
    m_qkv,
    m_attn_out,
    m_router,
    m_in,
    m_exp_out,
):
    rows, width = inputs.shape
    group_rows, top_count = expert_ids.shape
    experts, share, hidden = w_in.shape
    head_cols = w_attn_out.shape[0]
    heads = width // HD
    n_dp = lax.axis_size("dp")
    n_t = lax.axis_size("tensor")
    t_index = lax.axis_index("tensor")
    d_index = lax.axis_index("dp")
    per_host = max(1, experts // n_dp)
    copies = max(1, n_dp // experts)
    hosts = n_dp * per_host
    part = hidden // copies
    scale_qk = HD ** (-0.5)
    rows_pad = -(-rows // 16) * 16
    group_pad = n_t * rows_pad
    quarter = -(-(-(-CAP // n_t)) // 16) * 16
    slots = experts * quarter

    def padded(block):
        return jnp.pad(block, ((0, rows_pad - rows), (0, 0)))

    def group_of(block):
        return lax.all_gather(padded(block), "tensor", axis=0, tiled=True)

    def exchange(blocks, axis):
        return lax.all_to_all(blocks, axis, split_axis=0, concat_axis=0, tiled=True)

    def to_host(shard):
        parts = shard.reshape(experts, share, copies, part).transpose(0, 2, 1, 3)
        return exchange(parts.reshape(n_dp, per_host, share, part), "dp")

    def at_host(blocks):
        return blocks.transpose(1, 0, 2, 3).reshape(per_host, n_dp * share, part)

    def from_host(whole):
        blocks = whole.reshape(per_host, n_dp, share, part).transpose(1, 0, 2, 3)
        back = exchange(blocks, "dp").reshape(experts, copies, share, part)
        return back.transpose(0, 2, 1, 3).reshape(experts, share, copies * part)

    def pack_attention(three, out):
        return jnp.concatenate([three[0], three[1], three[2], out.T], axis=1)

    attn_weights = lax.all_gather(pack_attention(w_qkv, w_attn_out), "dp", axis=0, tiled=True)
    w_three, w_out_turned = attn_weights[:, : 3 * head_cols], attn_weights[:, 3 * head_cols :]
    w_exp_turned = jnp.swapaxes(w_exp_out, 1, 2)
    m_in_short = m_in.astype(BF)
    m_exp_short = jnp.swapaxes(m_exp_out.astype(BF), 1, 2)

    ids = expert_ids.reshape(n_t, rows, top_count)
    ids = jnp.pad(ids, ((0, 0), (0, rows_pad - rows), (0, 0)), constant_values=-1)
    ids = ids.reshape(group_pad, top_count)
    labels = lax.broadcasted_iota(jnp.int32, (group_pad, top_count, experts), 2)
    chosen = (ids[:, :, None] == labels).astype(F32)
    counted = jnp.sum(chosen, axis=1)
    earlier = (
        lax.broadcasted_iota(jnp.int32, (group_pad, group_pad), 0)
        > lax.broadcasted_iota(jnp.int32, (group_pad, group_pad), 1)
    ).astype(BF)
    before = mm("ts,se->te", earlier, counted.astype(BF))
    places = jnp.sum(before[:, None, :] * chosen, axis=2).astype(jnp.int32) - t_index * quarter
    mine = (places >= 0) & (places < quarter) & (ids >= 0)
    slot_of = jnp.where(mine, ids * quarter + places, -1)
    slot_rows = lax.broadcasted_iota(jnp.int32, (slots, group_pad), 0)
    picks = [slot_of[:, k][None, :] == slot_rows for k in range(top_count)]
    spread = sum(pick.astype(BF) for pick in picks)

    hidden_rows = inputs.astype(F32)
    first, first_normed, first_inverse = apply_layer_norm(
        hidden_rows, layer_norm_gains[0], layer_norm_biases[0]
    )
    act_one_group = group_of(first.astype(BF))
    cot_group = group_of(cotangent)
    images = rows // SEQ * n_t
    image_pad = group_pad // images

    def by_head(block):
        return block.reshape(images, image_pad, -1, HD)

    three = mm("td,dc->tc", act_one_group, w_three).astype(BF)
    query, key, value = [
        by_head(three[:, s * head_cols : (s + 1) * head_cols]) for s in range(3)
    ]
    scores = mm("bqhe,bkhe->bhqk", query, key) * scale_qk
    scores = jnp.where(lax.broadcasted_iota(jnp.int32, scores.shape, 3) < SEQ, scores, -1e30)
    expo = jnp.exp(scores - jnp.max(scores, axis=-1, keepdims=True))
    probs = expo / jnp.sum(expo, axis=-1, keepdims=True)
    probs_short = probs.astype(BF)
    mixed = mm("bhqk,bkhe->bqhe", probs_short, value).astype(BF).reshape(group_pad, head_cols)
    mixed = after(mixed, cot_group)
    attended = mm("te,de->td", mixed, w_out_turned).astype(BF)
    attended = lax.psum_scatter(attended, "tensor", scatter_dimension=0, tiled=True)
    middle = hidden_rows + attended[:rows].astype(F32)
    second, second_normed, second_inverse = apply_layer_norm(
        middle, layer_norm_gains[1], layer_norm_biases[1]
    )
    act_two = second.astype(BF)
    act_two_group = group_of(act_two)

    group_probs = jax.nn.softmax(mm("td,de->te", act_two_group, w_router), axis=-1)
    gates = jnp.sum(group_probs[:, None, :] * chosen, axis=2)
    gate_of_slot = sum(
        jnp.sum(jnp.where(pick, gates[:, k][None, :], 0.0), axis=1) for k, pick in enumerate(picks)
    )[:, None]
    slot_act = mm("st,td->sd", spread, act_two_group).astype(BF)
    cot_slot = mm("st,td->sd", spread, cot_group)
    slot_grad = (gate_of_slot * cot_slot).astype(BF)
    slot_pair = jnp.stack(
        [slot_act.reshape(experts, quarter, width), slot_grad.reshape(experts, quarter, width)], 1
    )
    if copies > 1:
        slot_pair = jnp.repeat(slot_pair, copies, axis=0)
    slot_pair = slot_pair.reshape(n_dp, per_host, 2, quarter, width)
    got = exchange(slot_pair, "dp")
    sent_in, sent_exp = to_host(w_in), to_host(w_exp_turned)
    sent_m_in, sent_m_exp = to_host(m_in_short), to_host(m_exp_short)
    host_in = at_host(sent_in)
    host_exp = at_host(sent_exp)
    in_grads, exp_grads, backs = [], [], []
    for e in range(per_host):
        e_rows, e_grad = [
            lax.all_gather(
                got[:, e, kind].reshape(n_dp * quarter, width), "tensor", axis=0, tiled=True
            )
            for kind in range(2)
        ]
        e_pre = mm("cd,df->cf", e_rows, host_in[e])
        normal = 0.5 * (1.0 + lax.erf(e_pre * INV_ROOT_TWO))
        slope = normal + e_pre * jnp.exp(-0.5 * e_pre * e_pre) * INV_ROOT_TWO_PI
        e_act = (e_pre * normal).astype(BF)
        e_grad_pre = (mm("cd,df->cf", e_grad, host_exp[e]) * slope).astype(BF)
        for part_sum in (
            mm("cf,df->cd", e_act, host_exp[e]),
            mm("cf,df->cd", e_grad_pre, host_in[e]),
        ):
            back = lax.psum_scatter(
                part_sum.astype(BF), "tensor", scatter_dimension=0, tiled=True
            )
            backs.append(back.reshape(n_dp, quarter, width))
        exp_grads.append(mm("cd,cf->df", e_grad, e_act))
        in_grads.append(mm("cd,cf->df", e_rows, e_grad_pre))
    host_in_grad, host_exp_grad = jnp.stack(in_grads), jnp.stack(exp_grads)

    back = jnp.stack(backs, axis=1)
    came = exchange(back, "dp").reshape(n_dp, per_host, 2, quarter, width)
    came = came.reshape(hosts // copies, copies, 2, quarter, width).astype(F32).sum(axis=1)
    moments = jnp.concatenate(
        [
            DECAY * at_host(sent_m_in).astype(F32) + host_in_grad,
            DECAY * at_host(sent_m_exp).astype(F32) + host_exp_grad,
        ],
        axis=0,
    ).astype(BF)
    in_grad = from_host(host_in_grad.astype(BF))
    exp_grad = from_host(host_exp_grad.astype(BF))
    members = [[e * copies + r for r in range(copies)] for e in range(n_dp // copies)]
    wide = lax.all_gather(moments, "tensor", axis=2, tiled=True)
    if copies > 1:
        wide = lax.all_gather(wide, "dp", axis=2, tiled=True, axis_index_groups=members)
    first_col = (lax.rem(d_index, copies) * n_t + t_index) * part
    own = [
        lax.dynamic_slice_in_dim(orthogonalize(wide[i]), first_col, part, 1)
        for i in range(2 * per_host)
    ]
    ortho = jnp.stack(own)

    slot_out = came[:, 0].reshape(slots, width)
    slot_row_grad = came[:, 1].reshape(slots, width).astype(BF)
    weighted = (gate_of_slot * slot_out).astype(BF)
    gate_grad_slot = jnp.sum(cot_slot * slot_out, axis=1)
    of_expert = (
        lax.broadcasted_iota(jnp.int32, (slots, 128), 0) // quarter
        == lax.broadcasted_iota(jnp.int32, (slots, 128), 1)
    )
    gate_grad_slot = jnp.where(of_expert, gate_grad_slot[:, None], 0.0).astype(BF)
    spread_cols = jnp.concatenate([weighted, slot_row_grad, gate_grad_slot], axis=1)
    token_part = mm("st,sc->tc", spread, spread_cols).astype(BF)
    token_sum = lax.psum_scatter(token_part, "tensor", scatter_dimension=0, tiled=True)
    token_sum = token_sum[:rows].astype(F32)
    output = (middle + token_sum[:, :width]).astype(BF)
    grad_probs = token_sum[:, 2 * width : 2 * width + experts]

    probs_local = jax.nn.softmax(mm("td,de->te", act_two, w_router), axis=-1)
    grad_logits = (
        probs_local * (grad_probs - jnp.sum(probs_local * grad_probs, axis=-1, keepdims=True))
    ).astype(BF)
    second_grad = token_sum[:, width : 2 * width] + mm("te,de->td", grad_logits, w_router)
    router_part = mm("td,te->ed", act_two, grad_logits)
    grad_mid_norm, gain_two_grad, bias_two_grad = norm_back(
        second_grad, second_normed, second_inverse, layer_norm_gains[1]
    )
    grad_middle = grad_mid_norm + cotangent.astype(F32)
    grad_mid_short = grad_middle.astype(BF)

    grad_mid_group = group_of(grad_mid_short)
    grad_heads = by_head(mm("td,de->te", grad_mid_group, w_out_turned).astype(BF))
    grad_weights = mm("bqhe,bkhe->bhqk", grad_heads, value)
    delta = jnp.sum(probs * grad_weights, axis=-1, keepdims=True)
    grad_scores = (probs * (grad_weights - delta)).astype(BF)
    grad_query = (mm("bhqk,bkhe->bqhe", grad_scores, key) * scale_qk).astype(BF)
    grad_key = (mm("bhqk,bqhe->bkhe", grad_scores, query) * scale_qk).astype(BF)
    grad_value = mm("bhqk,bqhe->bkhe", probs_short, grad_heads).astype(BF)
    grad_three = jnp.concatenate(
        [part.reshape(group_pad, head_cols) for part in (grad_query, grad_key, grad_value)], axis=1
    )
    first_grad = mm("tc,dc->td", grad_three, w_three).astype(BF)
    attn_grad = jnp.concatenate(
        [
            mm("td,tc->dc", act_one_group, grad_three).astype(BF),
            mm("td,tc->dc", grad_mid_group, mixed).astype(BF),
        ],
        axis=1,
    )
    attn_parts = exchange(attn_grad.reshape(n_dp, share, width), "dp")
    attn_sum = jnp.sum(attn_parts.astype(F32), axis=0)

    first_grad = lax.psum_scatter(first_grad, "tensor", scatter_dimension=0, tiled=True)
    grad_in_norm, gain_one_grad, bias_one_grad = norm_back(
        first_grad[:rows].astype(F32), first_normed, first_inverse, layer_norm_gains[0]
    )
    input_grad = grad_in_norm + grad_middle

    attn_moment = DECAY * pack_attention(m_qkv, m_attn_out) + attn_sum
    attn_blocks = attn_moment.reshape(share, 4, head_cols)
    qkv_moment_new = attn_blocks[:, :3].transpose(1, 0, 2)
    attn_out_moment_new = attn_blocks[:, 3].T
    vec_part = jnp.concatenate([gain_one_grad, gain_two_grad, bias_one_grad, bias_two_grad], 0)
    small_rows = -(-(4 + experts) // 8) * 8
    small_part = jnp.concatenate([vec_part, router_part], 0)
    small_part = jnp.pad(small_part, ((0, small_rows - 4 - experts), (0, 0)))
    gathered_dp = lax.all_gather(
        jnp.concatenate([attn_moment, small_part], 0).astype(BF), "dp", axis=0
    )
    small_part = jnp.sum(gathered_dp[:, share:].astype(F32), axis=0).astype(BF)
    gathered = jnp.concatenate([gathered_dp[:, :share].reshape(width, width), small_part], 0)
    gathered = lax.all_gather(gathered, "tensor", axis=0)
    small = jnp.sum(gathered[:, width:].astype(F32), axis=0)
    three_cols = 3 * head_cols
    last = gathered[n_t - 1, :width]
    packed_three = jnp.stack(
        [
            jnp.concatenate(
                [
                    gathered[b, :width, :three_cols],
                    last[:, b * head_cols : (b + 1) * head_cols],
                ],
                axis=1,
            )
            for b in range(3)
        ]
    )
    packed_out = jnp.concatenate([gathered[t, :width, three_cols:] for t in range(n_t)], axis=1)
    last_three, poly_three = ortho_call(packed_three)
    last_out, poly_out = ortho_call(packed_out[None])
    own_cols = jnp.where(
        t_index == n_t - 1,
        jnp.concatenate([last_three[b, :, three_cols:] for b in range(3)], axis=1),
        lax.dynamic_index_in_dim(last_three, jnp.minimum(t_index, 2), 0, False)[:, :three_cols],
    )
    own_rows = lax.dynamic_slice_in_dim(poly_three, d_index * share, share, 0)
    own_three = mm("ri,ic->rc", own_rows, own_cols)
    own_rows = lax.dynamic_slice_in_dim(poly_out, d_index * share, share, 0)
    own_cols = lax.dynamic_slice_in_dim(last_out[0], t_index * head_cols, head_cols, 1)
    own_out = mm("ri,ic->rc", own_rows, own_cols)
    own_qkv = own_three.reshape(share, 3, head_cols).transpose(1, 0, 2)
    qkv_new = w_qkv.astype(F32) - math.sqrt(3.0) * own_qkv
    attn_out_new = w_attn_out.astype(F32) - own_out.T

    norm_moment_new = DECAY * norm_moment + small[:4]
    norm_new = (
        jnp.concatenate([layer_norm_gains, layer_norm_biases], 0) - VEC_RATE * norm_moment_new
    )
    router_moment_turned = DECAY * m_router.T + small[4 : 4 + experts]
    router_moment_new = router_moment_turned.T
    router_new = w_router.astype(F32) - local_orthogonalize(router_moment_turned).T

    ortho_in, ortho_exp = from_host(ortho[:per_host]), from_host(ortho[per_host:])
    in_moment_new = DECAY * m_in + in_grad.astype(F32)
    exp_out_moment_new = DECAY * m_exp_out + jnp.swapaxes(exp_grad, 1, 2).astype(F32)
    in_new = w_in.astype(F32) - math.sqrt(max(1.0, FF / D)) * ortho_in.astype(F32)
    exp_out_new = w_exp_out.astype(F32) - jnp.swapaxes(ortho_exp, 1, 2).astype(F32)
    return (
        output,
        input_grad,
        norm_moment_new,
        norm_new,
        qkv_moment_new,
        qkv_new,
        attn_out_moment_new,
        attn_out_new,
        router_moment_new,
        router_new,
        in_moment_new,
        in_new,
        exp_out_moment_new,
        exp_out_new,
    )


def solution(mesh):
    both = P(("dp", "tensor"), None)
    cols = P(None, "dp", "tensor")
    turned = P(None, "tensor", "dp")
    in_specs = (
        both, both, P("dp", None), P(), P(), P(), cols, P("tensor", "dp"), P(), cols, turned,
        cols, P("tensor", "dp"), P(), cols, turned,
    )
    out_specs = (
        both, both, P(), P(), cols, cols, P("tensor", "dp"), P("tensor", "dp"), P(), P(),
        cols, cols, turned, turned,
    )
    n_dp, n_t = mesh.shape["dp"], mesh.shape["tensor"]
    whole = n_t == 4 and 2 * (EXPERTS // n_dp) == n_t and (D // n_dp) % 16 == 0
    step = local if whole else general
    return jax.shard_map(step, mesh=mesh, in_specs=in_specs, out_specs=out_specs, check_vma=False)
```
